512 devices in a mesh: ctx: 64 (over z, x, core), tp: 8 (over y).
Axes of the slice: x: 4, y: 8, z: 8, core: 2. Of those that a mesh axis runs over, the one named last changes fastest.
Arguments:
- queries: bfloat16 [256, 8192], P('tp', 'ctx'), may hold values from -9 to 9
- keys: bfloat16 [65536, 1024], P('ctx', 'tp'), may hold values from -6 to 6
- values: bfloat16 [65536, 1024], P('ctx', 'tp'), may hold values from -6 to 6
- counts: int32 [64], P('ctx'), may hold values from 1 to 1024, 49152 in all
- resp_len: int32 [1], replicated, may hold values from 128 to 256
Outputs:
- attended: bfloat16 [256, 8192], P('ctx', 'tp')
The draws below stay inside these ranges and needn't reach their ends.
Inputs may be any that keep to these rules, and one draw needn't show every extreme that they name: `counts`: the largest block count is exactly 1024; every block has at least one valid token.
All inputs are finite; a program needn't handle non-finite values.
Results may differ from the reference program's by a relative error of at most 0.0046.
Values may be sent and summed in bfloat16 or wider, within the bound.
No kernel may reach another device: no remote copies, remote signals or barrier semaphores. Data moves between devices by JAX's collectives and lax.ppermute only.
A program may use at most 64 MiB of HBM per device.

```python
import math
import jax
import jax.numpy as jnp
import numpy as np
from jax import lax

H = 64
KVH = 8
HS = 128
L = 1024
R = 256
NBLK = 64
KEYS = 65536


def draw_queries(key, part):
    key = jax.random.fold_in(key, 1)
    drawn = jnp.clip(jax.random.normal(key, (R, H * HS), jnp.float32), -6.0, 6.0)
    return drawn.astype(jnp.bfloat16)


def draw_keys(key, part):
    key = jax.random.fold_in(key, 2)
    drawn = jnp.clip(jax.random.normal(key, (KEYS, KVH * HS), jnp.float32), -6.0, 6.0)
    return drawn.astype(jnp.bfloat16)


def block_scale(stream_key, shape, pieces, least, high):
    loudness = 1.0
    for position, blocks in pieces:
        heights = jax.random.uniform(jax.random.fold_in(jax.random.fold_in(stream_key, 6), position), (blocks,), jnp.float32, least / len(pieces), high / len(pieces))
        loudness = loudness * jnp.repeat(jnp.exp(heights), shape[position] // blocks).reshape((-1,) + (1,) * (len(shape) - 1 - position))
    return loudness


def split_up(number_of, total, reach, skew):
    weights = [(1 << 20) // math.isqrt(standing ** skew) + 1 for standing in range(2, number_of + 1)]
    rest, given = total - reach - (number_of - 1), [1] * (number_of - 1)
    while rest > 0:
        candidates = [i for i in range(number_of - 1) if given[i] < reach]
        mass, remaining = sum([weights[i] for i in candidates]), rest
        for i in candidates:
            more = min(reach - given[i], max(1, remaining * weights[i] // mass), rest)
            given[i] = given[i] + more
            rest = rest - more
    return np.array([reach] + given)


def ragged(stream_key, amount, total, bound, lean):
    if amount == 2:
        one = jax.random.randint(stream_key, (), max(1, total - bound), min(bound, total - 1) + 1)
        return jnp.stack([one, total - one])
    sizes = jnp.asarray(split_up(amount, total, bound, lean), jnp.int32)
    couples = (amount - 1) // 2
    giver, taker = sizes[1:1 + 2 * couples:2], sizes[2:2 + 2 * couples:2]
    room = jnp.minimum(giver - 1, bound - taker)
    moved = jax.random.randint(jax.random.fold_in(stream_key, 1), (couples,), 0, 1 << 20) % (room + 1)
    sizes = sizes.at[1:1 + 2 * couples:2].set(giver - moved).at[2:2 + 2 * couples:2].set(taker + moved)
    return sizes[jax.random.permutation(jax.random.fold_in(stream_key, 2), amount)]


def bell_draw(key, shape, deviation, limit, cuts=(), held_as=jnp.bfloat16):
    values = deviation * jax.random.normal(key, shape, jnp.float32)
    if cuts:
        values = values * block_scale(key, shape, cuts, -0.22, 0.18)
    return jnp.clip(values, -limit, limit).astype(held_as)


def setup_inputs(seed: int = 0) -> dict:
    key_of = jax.random.split(jax.random.key(seed), 6)
    queries = draw_queries(jax.random.fold_in(key_of[5], 71), 0)
    keys = draw_keys(jax.random.fold_in(key_of[5], 71), 0)
    values = bell_draw(key_of[2], (KEYS, KVH * HS), 1.0, 6.0, ((0, 64), (1, 8)))
    counts = ragged(key_of[3], NBLK, NBLK * L * 3 // 4, L, 2).astype(jnp.int32)
    resp_len = jax.random.randint(key_of[4], (1,), R // 2, R + 1).astype(jnp.int32)
    return dict(queries=queries, keys=keys, values=values, counts=counts, resp_len=resp_len)


def reference(queries, keys, values, counts, resp_len):
    group_size = H // KVH
    score_scale = 1.0 / (HS ** 0.5)
    query_all = queries.astype(jnp.float32).reshape(R, KVH, group_size, HS)

    def one_block(state_now, index):
        numer, denom, peak_row = state_now
        key_blk = lax.dynamic_slice_in_dim(keys, index * L, L, 0).astype(jnp.float32).reshape(L, KVH, HS)
        val_blk = lax.dynamic_slice_in_dim(values, index * L, L, 0).astype(jnp.float32).reshape(L, KVH, HS)
        scores = jnp.einsum("rgqd,lgd->rgql", query_all, key_blk) * score_scale
        in_block = jnp.arange(L, dtype=jnp.int32) < counts[index]
        scores = jnp.where(in_block, scores, -jnp.inf)
        block_max = jnp.max(scores, axis=-1)
        weights = jnp.exp(scores - block_max[..., None]).astype(jnp.bfloat16)
        block_sum = jnp.sum(weights.astype(jnp.float32), axis=-1)
        block_out = jnp.einsum("rgql,lgd->rgqd", weights.astype(jnp.float32), val_blk)
        new_peak = jnp.maximum(peak_row, block_max)
        old_weight = jnp.exp(peak_row - new_peak)
        new_weight = jnp.exp(block_max - new_peak)
        numer = numer * old_weight[..., None] + block_out * new_weight[..., None]
        denom = denom * old_weight + block_sum * new_weight
        return (numer, denom, new_peak), None

    start = (jnp.zeros((R, KVH, group_size, HS), jnp.float32),
             jnp.zeros((R, KVH, group_size), jnp.float32),
             jnp.full((R, KVH, group_size), -jnp.inf, jnp.float32))
    final, _ = lax.scan(one_block, start, jnp.arange(NBLK, dtype=jnp.int32))
    numer, denom, _ = final
    result = (numer / denom[..., None]).reshape(R, H * HS)
    live = (jnp.arange(R, dtype=jnp.int32) < resp_len[0])[:, None]
    return jnp.where(live, result, 0.0).astype(jnp.bfloat16)
```

```python
import jax
import jax.numpy as jnp
from jax import lax
from jax.experimental import pallas as pl
from jax.experimental.pallas import tpu as pltpu
from jax.sharding import Mesh, PartitionSpec as P

HS = 128
LOG2E = 1.4426950408889634
EXP2_SCALE = LOG2E / HS**0.5
NZ, NX, NC, NY = 8, 4, 2, 8
SLOTS = 1024
SRC = NZ * NX
PAIRS = 32
SLOT_ROWS = 40
COUNT_BASE = 64
MASKED = -1e30


def lane_ids(shape):
    return lax.broadcasted_iota(jnp.int32, shape, len(shape) - 1)


def attend_kernel(count_ref, q_ref, key_ref, value_ref, got_ref, out_ref, wide_ref):
    ones = jnp.ones((SLOTS, HS), jnp.bfloat16)
    for block, rows in enumerate((value_ref[...], got_ref[SLOTS : 2 * SLOTS, :])):
        wide_ref[block, :, :HS] = rows
        wide_ref[block, :, HS:] = ones
    slot = lane_ids((1, SLOTS))
    tail = got_ref[2 * SLOTS + 16 : 2 * SLOTS + 32, :].astype(jnp.float32)
    got_count = tail[0:1] * COUNT_BASE + tail[1:2]
    got_count = jnp.concatenate([got_count] * (SLOTS // HS), axis=1).astype(jnp.int32)
    biases = (
        jnp.where(slot < count_ref[0], 0.0, MASKED),
        jnp.where(slot < got_count, 0.0, MASKED),
    )

    tile = 2 * NX * PAIRS
    pair = lax.broadcasted_iota(jnp.int32, (8, PAIRS, HS), 1)
    lane = lane_ids((8, PAIRS, HS))
    diagonal = (lane % PAIRS) == pair
    part = lane // PAIRS
    sub = lax.broadcasted_iota(jnp.int32, (8, 8, HS), 1)

    def by_slot(x):
        return jnp.swapaxes(x.reshape(NX, 2, NX, 8, HS), 0, 1).swapaxes(1, 2).reshape(8, PAIRS, HS)

    for step in range(NY // 2):
        q = q_ref[:, 2 * step : 2 * step + 2].reshape(tile, HS)
        found = []
        for block in range(2):
            keys = key_ref[...] if block == 0 else got_ref[:SLOTS, :]
            scores = lax.dot_general(
                q, keys, (((1,), (1,)), ((), ())), preferred_element_type=jnp.float32
            )
            scores = scores + biases[block]
            peak = jnp.max(scores, axis=1, keepdims=True)
            weights = jnp.exp2((scores - peak) * EXP2_SCALE).astype(jnp.bfloat16)
            both = jnp.dot(weights, wide_ref[block], preferred_element_type=jnp.float32)
            found.append((both[:, :HS], both[:, HS:], peak))
        (out0, sum0, peak0), (out1, sum1, peak1) = found
        ref = jnp.maximum(peak0, peak1).astype(jnp.bfloat16).astype(jnp.float32)
        scale0 = jnp.exp2((peak0 - ref) * EXP2_SCALE)
        scale1 = jnp.exp2((peak1 - ref) * EXP2_SCALE)
        out = by_slot(out0 * scale0 + out1 * scale1)
        total = by_slot(sum0 * scale0 + sum1 * scale1)
        ref = by_slot(jnp.broadcast_to(ref, (tile, HS)))
        high = total.astype(jnp.bfloat16).astype(jnp.float32)
        stats = jnp.where(part == 0, ref, jnp.where(part == 1, high, total - high))
        stats = jnp.where(diagonal & (part < 3), stats, 0.0)
        stats = jnp.sum(stats, axis=1, keepdims=True)
        stats = jnp.where(sub == 0, stats, 0.0)
        full = jnp.concatenate([out, stats], axis=1).reshape(8 * SLOT_ROWS, HS)
        out_ref[8 * SLOT_ROWS * step : 8 * SLOT_ROWS * (step + 1), :] = full.astype(jnp.bfloat16)


def merge_kernel(live_ref, parts_ref, out_ref):
    parts = parts_ref[...].astype(jnp.float32).reshape(SRC, SLOT_ROWS, HS)
    stats = parts[:, PAIRS, :]
    stats = jnp.concatenate([stats, jnp.zeros((HS - SRC, HS), jnp.float32)], axis=0).T
    valid = lane_ids((PAIRS, HS)) < SRC
    peaks = jnp.where(valid, stats[:PAIRS], -jnp.inf)
    sums = stats[PAIRS : 2 * PAIRS] + stats[2 * PAIRS : 3 * PAIRS]
    peak = jnp.max(peaks, axis=1, keepdims=True)
    scale = jnp.exp2((peaks - peak) * EXP2_SCALE)
    denom = jnp.sum(scale * sums, axis=1, keepdims=True)
    numer = parts[0, :PAIRS] * scale[:, 0:1]
    for src in range(1, SRC):
        numer = numer + parts[src, :PAIRS] * scale[:, src : src + 1]
    result = numer / denom
    rows = PAIRS // 8
    row = lax.broadcasted_iota(jnp.int32, (rows, HS), 0)
    live = row < live_ref[0]
    for head in range(8):
        block = result[rows * head : rows * (head + 1)]
        out_ref[:, HS * head : HS * (head + 1)] = jnp.where(live, block, 0.0).astype(jnp.bfloat16)


def local(queries, keys, values, counts, resp_len):
    core = lax.axis_index("core")
    with jax.named_scope("pair_exchange"):
        halves = queries.reshape(NX, NC, 4, HS)
        first, second = halves[:, 0], halves[:, 1]
        own = jnp.where(core == 0, first, second)
        other = jnp.where(core == 0, second, first).reshape(16, HS)
        count_rows = jnp.stack([counts[0] // COUNT_BASE, counts[0] % COUNT_BASE])
        count_rows = jnp.broadcast_to(count_rows[:, None].astype(jnp.bfloat16), (2, HS))
        tail = jnp.concatenate([count_rows, jnp.zeros((14, HS), jnp.bfloat16)], axis=0)
        send = jnp.concatenate([keys, values, other, tail], axis=0)
        got = lax.ppermute(send, "core", [(0, 1), (1, 0)])
        theirs = got[2 * SLOTS : 2 * SLOTS + 16].reshape(NX, 4, HS)
        block = jnp.stack(
            [jnp.where(core == 0, own, theirs), jnp.where(core == 0, theirs, own)], axis=1
        ).reshape(PAIRS, HS)
    with jax.named_scope("query_spread"):
        groups = lax.all_to_all(
            jnp.broadcast_to(block[None], (NZ, PAIRS, HS)), "z", 0, 0, tiled=True
        )
        groups = jnp.broadcast_to(groups[None], (NX, NY, PAIRS, HS)).reshape(SRC, PAIRS, HS)
        spread = lax.all_to_all(groups, ("x", "tp"), 0, 0, tiled=True)
        spread = spread.reshape(NX, NY, PAIRS, HS)
    vmem = pl.BlockSpec(memory_space=pltpu.VMEM)
    smem = pl.BlockSpec(memory_space=pltpu.SMEM)
    with jax.named_scope("attend"):
        parts = pl.pallas_call(
            attend_kernel,
            out_shape=jax.ShapeDtypeStruct((SRC * SLOT_ROWS, HS), jnp.bfloat16),
            in_specs=[smem, vmem, vmem, vmem, vmem],
            out_specs=vmem,
            scratch_shapes=[pltpu.VMEM((2, SLOTS, 2 * HS), jnp.bfloat16)],
            compiler_params=pltpu.CompilerParams(vmem_limit_bytes=32 * 2**20),
        )(counts, spread, keys, values, got)
    with jax.named_scope("merge"):
        parts = lax.all_to_all(
            parts.reshape(SRC, SLOT_ROWS, HS), ("z", "x"), 0, 0, tiled=True
        ).reshape(SRC * SLOT_ROWS, HS)
        index = lax.axis_index(("z", "x", "core"))
        live = resp_len - index * 4
        return pl.pallas_call(
            merge_kernel,
            out_shape=jax.ShapeDtypeStruct((4, 8 * HS), jnp.bfloat16),
            in_specs=[smem, vmem],
            out_specs=vmem,
            compiler_params=pltpu.CompilerParams(vmem_limit_bytes=32 * 2**20),
        )(live, parts)


def solution(mesh):
    grid = Mesh(mesh.devices.reshape(NZ, NX, NC, NY), ("z", "x", "core", "tp"))
    ctx = ("z", "x", "core")
    in_specs = (P("tp", ctx), P(ctx, "tp"), P(ctx, "tp"), P(ctx), P())
    return jax.shard_map(
        local, mesh=grid, in_specs=in_specs, out_specs=P(ctx, "tp"), check_vma=False
    )
```

```python
import jax
import jax.numpy as jnp
from jax import lax
from jax.experimental import pallas as pl
from jax.experimental.pallas import tpu as pltpu
from jax.sharding import Mesh, PartitionSpec as P

HS = 128
LOG2E = 1.4426950408889634
EXP2_SCALE = LOG2E / HS**0.5
NZ, NX, NC, NY = 8, 4, 2, 8
SLOTS = 1024
SRC = NZ * NX
PAIRS = 32
SLOT_ROWS = 40
SEND_ROWS = 2 * SLOTS + 16
COUNT_BASE = 64
MASKED = -1e30


def lane_ids(shape):
    return lax.broadcasted_iota(jnp.int32, shape, len(shape) - 1)


def interleave(first, second):
    low = jnp.concatenate([first[:, :4], second[:, :4]], axis=1)
    high = jnp.concatenate([first[:, 4:], second[:, 4:]], axis=1)
    return low, high


def pack_kernel(count_ref, query_ref, key_ref, value_ref, send_ref, slots_ref, rows_ref, sems):
    copies = [
        pltpu.make_async_copy(query_ref, rows_ref, sems.at[2]),
        pltpu.make_async_copy(key_ref, send_ref.at[pl.ds(0, SLOTS)], sems.at[0]),
        pltpu.make_async_copy(value_ref, send_ref.at[pl.ds(SLOTS, SLOTS)], sems.at[1]),
    ]
    for copy in copies:
        copy.start()
    count = count_ref[0]
    high = count // COUNT_BASE
    row = lax.broadcasted_iota(jnp.int32, (16, HS), 0)
    tail = jnp.where(row == 0, high, count - high * COUNT_BASE)
    send_ref[2 * SLOTS : SEND_ROWS, :] = tail.astype(jnp.float32).astype(jnp.bfloat16)
    copies[0].wait()
    rows = rows_ref[...].astype(jnp.float32).reshape(2, 2, 8, HS)
    for core, half in enumerate(interleave(rows[:, 0], rows[:, 1])):
        half = half.reshape(16, HS).astype(jnp.bfloat16)
        for z in range(NZ):
            slots_ref[z, core] = half
    for copy in copies[1:]:
        copy.wait()


def attend_kernel(count_ref, q_ref, key_ref, value_ref, got_ref, out_ref, wide_ref):
    ones = jnp.ones((SLOTS, HS), jnp.bfloat16)
    for block, rows in enumerate((value_ref[...], got_ref[SLOTS : 2 * SLOTS, :])):
        wide_ref[block, :, :HS] = rows
        wide_ref[block, :, HS:] = ones
    slot = lane_ids((1, SLOTS))
    tail = got_ref[2 * SLOTS : SEND_ROWS, :].astype(jnp.float32)
    got_count = tail[0:1] * COUNT_BASE + tail[1:2]
    got_count = jnp.concatenate([got_count] * (SLOTS // HS), axis=1).astype(jnp.int32)
    biases = (
        jnp.where(slot < count_ref[0], 0.0, MASKED),
        jnp.where(slot < got_count, 0.0, MASKED),
    )

    tile = 2 * NX * PAIRS
    part = lane_ids((tile, HS)) // PAIRS
    pair = lax.broadcasted_iota(jnp.int32, (8, PAIRS, HS), 1)
    lane = lane_ids((8, PAIRS, HS))
    diagonal = (lane % PAIRS == pair) & (lane < 3 * PAIRS)
    sub = lax.broadcasted_iota(jnp.int32, (8, 8, HS), 1)

    def by_slot(x):
        x = x.reshape(NX * 2, 2, 2, 8, HS)
        low, high = interleave(x[:, 0].reshape(-1, 8, HS), x[:, 1].reshape(-1, 8, HS))
        x = jnp.stack([low, high], axis=1).reshape(NX, 8, 8, HS)
        return jnp.swapaxes(x, 0, 1).reshape(8, PAIRS, HS)

    for step in range(NY // 2):
        q = q_ref[:, 2 * step : 2 * step + 2].reshape(tile, HS)
        found = []
        for block in range(2):
            keys = key_ref[...] if block == 0 else got_ref[:SLOTS, :]
            scores = lax.dot_general(
                q, keys, (((1,), (1,)), ((), ())), preferred_element_type=jnp.float32
            )
            scores = scores + biases[block]
            peak = jnp.max(scores, axis=1, keepdims=True)
            weights = jnp.exp2((scores - peak) * EXP2_SCALE).astype(jnp.bfloat16)
            both = jnp.dot(weights, wide_ref[block], preferred_element_type=jnp.float32)
            found.append((both[:, :HS], both[:, HS:], peak))
        (out0, sum0, peak0), (out1, sum1, peak1) = found
        ref = jnp.maximum(peak0, peak1).astype(jnp.bfloat16).astype(jnp.float32)
        scale0 = jnp.exp2((peak0 - ref) * EXP2_SCALE)
        scale1 = jnp.exp2((peak1 - ref) * EXP2_SCALE)
        out = by_slot(out0 * scale0 + out1 * scale1)
        total = sum0 * scale0 + sum1 * scale1
        high = total.astype(jnp.bfloat16).astype(jnp.float32)
        stats = jnp.where(part == 0, ref, jnp.where(part == 1, high, total - high))
        stats = jnp.where(diagonal, by_slot(stats), 0.0)
        stats = jnp.sum(stats, axis=1, keepdims=True)
        stats = jnp.where(sub == 0, stats, 0.0)
        full = jnp.concatenate([out, stats], axis=1).reshape(8 * SLOT_ROWS, HS)
        out_ref[8 * SLOT_ROWS * step : 8 * SLOT_ROWS * (step + 1), :] = full.astype(jnp.bfloat16)


def merge_kernel(resp_ref, parts_ref, out_ref):
    parts = parts_ref[...].astype(jnp.float32).reshape(SRC, SLOT_ROWS, HS)
    stats = parts[:, PAIRS, :]
    stats = jnp.concatenate([stats, jnp.zeros((HS - SRC, HS), jnp.float32)], axis=0).T
    valid = lane_ids((PAIRS, HS)) < SRC
    peaks = jnp.where(valid, stats[:PAIRS], -jnp.inf)
    sums = stats[PAIRS : 2 * PAIRS] + stats[2 * PAIRS : 3 * PAIRS]
    peak = jnp.max(peaks, axis=1, keepdims=True)
    scale = jnp.exp2((peaks - peak) * EXP2_SCALE)
    denom = jnp.sum(scale * sums, axis=1, keepdims=True)
    numer = parts[0, :PAIRS] * scale[:, 0:1]
    for src in range(1, SRC):
        numer = numer + parts[src, :PAIRS] * scale[:, src : src + 1]
    result = numer / denom
    rows = PAIRS // 8
    row = lax.broadcasted_iota(jnp.int32, (rows, HS), 0)
    live = row < resp_ref[0] - rows * lax.axis_index(("z", "x", "core"))
    for head in range(8):
        block = result[rows * head : rows * (head + 1)]
        out_ref[:, HS * head : HS * (head + 1)] = jnp.where(live, block, 0.0).astype(jnp.bfloat16)


VMEM = pl.BlockSpec(memory_space=pltpu.VMEM)
SMEM = pl.BlockSpec(memory_space=pltpu.SMEM)
HBM = pl.BlockSpec(memory_space=pltpu.HBM)


def pack(counts, queries, keys, values):
    return pl.pallas_call(
        pack_kernel,
        out_shape=(
            jax.ShapeDtypeStruct((SEND_ROWS, HS), jnp.bfloat16),
            jax.ShapeDtypeStruct((NZ, NC, 16, HS), jnp.bfloat16),
        ),
        in_specs=[SMEM, HBM, HBM, HBM],
        out_specs=(VMEM, VMEM),
        scratch_shapes=[pltpu.VMEM((PAIRS, HS), jnp.bfloat16), pltpu.SemaphoreType.DMA((3,))],
        compiler_params=pltpu.CompilerParams(vmem_limit_bytes=4 * 2**20),
    )(counts, queries, keys, values)


def attend(counts, spread, keys, values, got):
    return pl.pallas_call(
        attend_kernel,
        out_shape=jax.ShapeDtypeStruct((SRC * SLOT_ROWS, HS), jnp.bfloat16),
        in_specs=[SMEM, VMEM, VMEM, VMEM, VMEM],
        out_specs=VMEM,
        scratch_shapes=[pltpu.VMEM((2, SLOTS, 2 * HS), jnp.bfloat16)],
        compiler_params=pltpu.CompilerParams(vmem_limit_bytes=12 * 2**20),
    )(counts, spread, keys, values, got)


def merge(resp_len, parts):
    return pl.pallas_call(
        merge_kernel,
        out_shape=jax.ShapeDtypeStruct((4, 8 * HS), jnp.bfloat16),
        in_specs=[SMEM, VMEM],
        out_specs=VMEM,
        compiler_params=pltpu.CompilerParams(vmem_limit_bytes=4 * 2**20),
    )(resp_len, parts)


def local(queries, keys, values, counts, resp_len):
    with jax.named_scope("pair_exchange"):
        send, slots = pack(counts, queries, keys, values)
        got = lax.ppermute(send, "core", [(0, 1), (1, 0)])
    with jax.named_scope("query_spread"):
        groups = lax.all_to_all(
            slots.reshape(NZ * NC, 16, HS), ("z", "core"), 0, 0, tiled=True
        ).reshape(NZ, PAIRS, HS)
        groups = jnp.broadcast_to(groups[None], (NX, NY, PAIRS, HS)).reshape(SRC, PAIRS, HS)
        spread = lax.all_to_all(groups, ("x", "tp"), 0, 0, tiled=True)
        spread = spread.reshape(NX, NY, PAIRS, HS)
    with jax.named_scope("attend"):
        parts = attend(counts, spread, keys, values, got)
    with jax.named_scope("merge"):
        parts = lax.all_to_all(
            parts.reshape(SRC, SLOT_ROWS, HS), ("z", "x"), 0, 0, tiled=True
        ).reshape(SRC * SLOT_ROWS, HS)
        return merge(resp_len, parts)


def solution(mesh):
    grid = Mesh(mesh.devices.reshape(NZ, NX, NC, NY), ("z", "x", "core", "tp"))
    ctx = ("z", "x", "core")
    in_specs = (P("tp", ctx), P(ctx, "tp"), P(ctx, "tp"), P(ctx), P())
    return jax.shard_map(
        local, mesh=grid, in_specs=in_specs, out_specs=P(ctx, "tp"), check_vma=False
    )
```

```python
import jax
import jax.numpy as jnp
from jax import lax
from jax.experimental import pallas as pl
from jax.experimental.pallas import tpu as pltpu
from jax.sharding import Mesh, PartitionSpec as P

HS = 128
LOG2E = 1.4426950408889634
EXP2_SCALE = LOG2E / HS**0.5
NZ, NX, NC, NY = 8, 4, 2, 8
SLOTS = 1024
SRC = NZ * NX
PAIRS = 32
SLOT_ROWS = 40
SEND_ROWS = 2 * SLOTS + 16
COUNT_BASE = 64
MASKED = -1e30


def lane_ids(shape):
    return lax.broadcasted_iota(jnp.int32, shape, len(shape) - 1)


def interleave(first, second):
    low = jnp.concatenate([first[:, :4], second[:, :4]], axis=1)
    high = jnp.concatenate([first[:, 4:], second[:, 4:]], axis=1)
    return low, high


def pack_kernel(query_ref, key_ref, value_ref, count_ref, resp_ref, slots_ref, send_ref):
    rows = query_ref[...].astype(jnp.float32).reshape(2, 2, 8, HS)
    for core, half in enumerate(interleave(rows[:, 0], rows[:, 1])):
        half = half.reshape(16, HS).astype(jnp.bfloat16)
        for z in range(NZ):
            slots_ref[z, core] = half
    count = count_ref[...]
    row = lax.broadcasted_iota(jnp.int32, (16, HS), 0)
    high = count // COUNT_BASE
    tail = jnp.where(row == 0, high, jnp.where(row == 1, count - high * COUNT_BASE, resp_ref[...]))
    send_ref[:SLOTS, :] = key_ref[...]
    send_ref[SLOTS : 2 * SLOTS, :] = value_ref[...]
    send_ref[2 * SLOTS : SEND_ROWS, :] = tail.astype(jnp.float32).astype(jnp.bfloat16)


def widen_kernel(own_ref, _, wide_ref):
    wide_ref[:, :HS] = own_ref[SLOTS : 2 * SLOTS, :]
    wide_ref[:, HS:] = jnp.ones((SLOTS, HS), jnp.bfloat16)


def attend_kernel(q_ref, own_ref, own_wide_ref, got_ref, out_ref, wide_ref):
    wide_ref[:, :HS] = got_ref[SLOTS : 2 * SLOTS, :]
    wide_ref[:, HS:] = jnp.ones((SLOTS, HS), jnp.bfloat16)
    slot = lane_ids((1, SLOTS))
    biases = []
    for ref in (own_ref, got_ref):
        tail = ref[2 * SLOTS : SEND_ROWS, :].astype(jnp.float32)
        count = tail[0:1] * COUNT_BASE + tail[1:2]
        count = jnp.concatenate([count] * (SLOTS // HS), axis=1).astype(jnp.int32)
        biases.append(jnp.where(slot < count, 0.0, MASKED))
    resp = tail[2:3]

    tile = 2 * NX * PAIRS
    part = lane_ids((tile, HS)) // PAIRS
    pair = lax.broadcasted_iota(jnp.int32, (8, PAIRS, HS), 1)
    lane = lane_ids((8, PAIRS, HS))
    diagonal = lane % PAIRS == pair
    sub = lax.broadcasted_iota(jnp.int32, (8, 8, HS), 1)

    def by_slot(x):
        x = x.reshape(NX * 2, 2, 2, 8, HS)
        low, high = interleave(x[:, 0].reshape(-1, 8, HS), x[:, 1].reshape(-1, 8, HS))
        x = jnp.stack([low, high], axis=1).reshape(NX, 8, 8, HS)
        return jnp.swapaxes(x, 0, 1).reshape(8, PAIRS, HS)

    for step in range(NY // 2):
        q = q_ref[:, 2 * step : 2 * step + 2].reshape(tile, HS)
        found = []
        for block, (keys_ref, values_ref) in enumerate(((own_ref, own_wide_ref), (got_ref, wide_ref))):
            keys = keys_ref[:SLOTS, :]
            scores = lax.dot_general(
                q, keys, (((1,), (1,)), ((), ())), preferred_element_type=jnp.float32
            )
            scores = scores + biases[block]
            peak = jnp.max(scores, axis=1, keepdims=True)
            weights = jnp.exp2((scores - peak) * EXP2_SCALE).astype(jnp.bfloat16)
            both = jnp.dot(weights, values_ref[...], preferred_element_type=jnp.float32)
            found.append((both[:, :HS], both[:, HS:], peak))
        (out0, sum0, peak0), (out1, sum1, peak1) = found
        ref = jnp.maximum(peak0, peak1).astype(jnp.bfloat16).astype(jnp.float32)
        scale0 = jnp.exp2((peak0 - ref) * EXP2_SCALE)
        scale1 = jnp.exp2((peak1 - ref) * EXP2_SCALE)
        out = by_slot(out0 * scale0 + out1 * scale1)
        total = sum0 * scale0 + sum1 * scale1
        high = total.astype(jnp.bfloat16).astype(jnp.float32)
        stats = jnp.where(part == 1, high, jnp.where(part == 2, total - high, resp))
        stats = jnp.where(part == 0, ref, stats)
        stats = jnp.where(diagonal, by_slot(stats), 0.0)
        stats = jnp.sum(stats, axis=1, keepdims=True)
        stats = jnp.where(sub == 0, stats, 0.0)
        full = jnp.concatenate([out, stats], axis=1).reshape(8 * SLOT_ROWS, HS)
        out_ref[8 * SLOT_ROWS * step : 8 * SLOT_ROWS * (step + 1), :] = full.astype(jnp.bfloat16)


def merge_kernel(parts_ref, out_ref):
    parts = parts_ref[...].astype(jnp.float32).reshape(SRC, SLOT_ROWS, HS)
    resp = parts[0, PAIRS : PAIRS + 1, 3 * PAIRS : 3 * PAIRS + 1].astype(jnp.int32)
    stats = parts[:, PAIRS, :]
    stats = jnp.concatenate([stats, jnp.zeros((HS - SRC, HS), jnp.float32)], axis=0).T
    valid = lane_ids((PAIRS, HS)) < SRC
    peaks = jnp.where(valid, stats[:PAIRS], -jnp.inf)
    sums = stats[PAIRS : 2 * PAIRS] + stats[2 * PAIRS : 3 * PAIRS]
    peak = jnp.max(peaks, axis=1, keepdims=True)
    scale = jnp.exp2((peaks - peak) * EXP2_SCALE)
    denom = jnp.sum(scale * sums, axis=1, keepdims=True)
    numer = parts[0, :PAIRS] * scale[:, 0:1]
    for src in range(1, SRC):
        numer = numer + parts[src, :PAIRS] * scale[:, src : src + 1]
    result = numer / denom
    rows = PAIRS // 8
    row = lax.broadcasted_iota(jnp.int32, (rows, HS), 0)
    live = row + rows * lax.axis_index(("z", "x", "core")) < resp
    for head in range(8):
        block = result[rows * head : rows * (head + 1)]
        out_ref[:, HS * head : HS * (head + 1)] = jnp.where(live, block, 0.0).astype(jnp.bfloat16)


VMEM = pl.BlockSpec(memory_space=pltpu.VMEM)
HBM = pl.BlockSpec(memory_space=pltpu.HBM)


def pack(queries, keys, values, counts, resp_len):
    return pl.pallas_call(
        pack_kernel,
        out_shape=(
            jax.ShapeDtypeStruct((NZ, NC, 16, HS), jnp.bfloat16),
            jax.ShapeDtypeStruct((SEND_ROWS, HS), jnp.bfloat16),
        ),
        in_specs=[VMEM] * 5,
        out_specs=(VMEM, VMEM),
        compiler_params=pltpu.CompilerParams(vmem_limit_bytes=60 * 2**20),
    )(queries, keys, values, counts.reshape(1, 1), resp_len.reshape(1, 1))


def widen(own, after):
    return pl.pallas_call(
        widen_kernel,
        out_shape=jax.ShapeDtypeStruct((SLOTS, 2 * HS), jnp.bfloat16),
        in_specs=[VMEM, HBM],
        out_specs=VMEM,
        compiler_params=pltpu.CompilerParams(vmem_limit_bytes=2**20),
    )(own, after)


def attend(spread, own, wide, got):
    return pl.pallas_call(
        attend_kernel,
        out_shape=jax.ShapeDtypeStruct((SRC * SLOT_ROWS, HS), jnp.bfloat16),
        in_specs=[VMEM, VMEM, VMEM, VMEM],
        out_specs=VMEM,
        scratch_shapes=[pltpu.VMEM((SLOTS, 2 * HS), jnp.bfloat16)],
        compiler_params=pltpu.CompilerParams(vmem_limit_bytes=12 * 2**20),
    )(spread, own, wide, got)


def merge(parts):
    return pl.pallas_call(
        merge_kernel,
        out_shape=jax.ShapeDtypeStruct((4, 8 * HS), jnp.bfloat16),
        in_specs=[VMEM],
        out_specs=VMEM,
        compiler_params=pltpu.CompilerParams(vmem_limit_bytes=4 * 2**20),
    )(parts)


def local(queries, keys, values, counts, resp_len):
    with jax.named_scope("query_spread"):
        slots, own = pack(queries, keys, values, counts, resp_len)
        halves = slots.reshape(NZ * NC, 16, HS)
        groups = lax.all_to_all(halves, ("z", "core"), 0, 0, tiled=True).reshape(NZ, PAIRS, HS)
    with jax.named_scope("pair_exchange"):
        got = lax.ppermute(own, "core", [(0, 1), (1, 0)])
    groups, own = lax.optimization_barrier((groups, own))
    with jax.named_scope("query_spread"):
        groups = jnp.broadcast_to(groups[None], (NX, NY, PAIRS, HS)).reshape(SRC, PAIRS, HS)
        spread = lax.all_to_all(groups, ("x", "tp"), 0, 0, tiled=True)
        spread = spread.reshape(NX, NY, PAIRS, HS)
    with jax.named_scope("attend"):
        wide = widen(own, spread)
        parts = attend(spread, own, wide, got)
    with jax.named_scope("merge"):
        parts = lax.all_to_all(
            parts.reshape(SRC, SLOT_ROWS, HS), ("z", "x"), 0, 0, tiled=True
        ).reshape(SRC * SLOT_ROWS, HS)
        return merge(parts)


def solution(mesh):
    grid = Mesh(mesh.devices.reshape(NZ, NX, NC, NY), ("z", "x", "core", "tp"))
    ctx = ("z", "x", "core")
    in_specs = (P("tp", ctx), P(ctx, "tp"), P(ctx, "tp"), P(ctx), P())
    return jax.shard_map(
        local, mesh=grid, in_specs=in_specs, out_specs=P(ctx, "tp"), check_vma=False
    )
```

```python
import jax
import jax.numpy as jnp
from jax import lax
from jax.experimental import pallas as pl
from jax.experimental.pallas import tpu as pltpu
from jax.sharding import Mesh, PartitionSpec as P

HS = 128
LOG2E = 1.4426950408889634
EXP2_SCALE = LOG2E / HS**0.5
NZ, NX, NC, NY = 8, 4, 2, 8
SLOTS = 1024
SRC = NZ * NX
PAIRS = 32
SLOT_ROWS = 40
SEND_ROWS = 2 * SLOTS + 16
COUNT_BASE = 64
FIRST_X, FIRST_YZ = 2, 4
MASKED = -1e30


def lane_ids(shape):
    return lax.broadcasted_iota(jnp.int32, shape, len(shape) - 1)


def device(z, x, core, y):
    return ((z % NZ * NX + x % NX) * NC + core) * NY + y % NY


def groups_zc():
    return [
        [device(z + FIRST_YZ, x, core, y) for z in range(NZ) for core in range(NC)]
        for x in range(NX)
        for y in range(NY)
    ]


def groups_xy():
    return [
        [device(z, x + FIRST_X, core, y + FIRST_YZ) for x in range(NX) for y in range(NY)]
        for z in range(NZ)
        for core in range(NC)
    ]


def groups_zx():
    return [
        [device(z + FIRST_YZ, x + FIRST_X, core, y) for z in range(NZ) for x in range(NX)]
        for core in range(NC)
        for y in range(NY)
    ]


def exchange(blocks, groups):
    axes = ("z", "x", "core", "tp")
    return lax.all_to_all(blocks, axes, 0, 0, axis_index_groups=groups, tiled=True)


def interleave(first, second):
    low = jnp.concatenate([first[:, :4], second[:, :4]], axis=1)
    high = jnp.concatenate([first[:, 4:], second[:, 4:]], axis=1)
    return low, high


def pack_kernel(query_ref, key_ref, value_ref, count_ref, resp_ref, slots_ref, send_ref):
    rows = query_ref[...].astype(jnp.float32).reshape(2, 2, 8, HS)
    for core, half in enumerate(interleave(rows[:, 0], rows[:, 1])):
        half = half.reshape(16, HS).astype(jnp.bfloat16)
        for z in range(NZ):
            slots_ref[z, core] = half
    count = count_ref[...]
    row = lax.broadcasted_iota(jnp.int32, (16, HS), 0)
    high = count // COUNT_BASE
    tail = jnp.where(row == 0, high, jnp.where(row == 1, count - high * COUNT_BASE, resp_ref[...]))
    send_ref[:SLOTS, :] = key_ref[...]
    send_ref[SLOTS : 2 * SLOTS, :] = value_ref[...]
    send_ref[2 * SLOTS : SEND_ROWS, :] = tail.astype(jnp.float32).astype(jnp.bfloat16)


def widen_kernel(own_ref, _, wide_ref):
    wide_ref[:, :HS] = own_ref[SLOTS : 2 * SLOTS, :]
    wide_ref[:, HS:] = jnp.ones((SLOTS, HS), jnp.bfloat16)


def attend_kernel(q_ref, own_ref, own_wide_ref, got_ref, out_ref, wide_ref):
    wide_ref[:, :HS] = got_ref[SLOTS : 2 * SLOTS, :]
    wide_ref[:, HS:] = jnp.ones((SLOTS, HS), jnp.bfloat16)
    slot = lane_ids((1, SLOTS))
    biases = []
    for ref in (own_ref, got_ref):
        tail = ref[2 * SLOTS : SEND_ROWS, :].astype(jnp.float32)
        count = tail[0:1] * COUNT_BASE + tail[1:2]
        count = jnp.concatenate([count] * (SLOTS // HS), axis=1).astype(jnp.int32)
        biases.append(jnp.where(slot < count, 0.0, MASKED))
    resp = tail[2:3]

    tile = 2 * NX * PAIRS
    part = lane_ids((tile, HS)) // PAIRS
    pair = lax.broadcasted_iota(jnp.int32, (8, PAIRS, HS), 1)
    lane = lane_ids((8, PAIRS, HS))
    diagonal = lane % PAIRS == pair
    sub = lax.broadcasted_iota(jnp.int32, (8, 8, HS), 1)

    def by_slot(x):
        x = x.reshape(NX * 2, 2, 2, 8, HS)
        low, high = interleave(x[:, 0].reshape(-1, 8, HS), x[:, 1].reshape(-1, 8, HS))
        x = jnp.stack([low, high], axis=1).reshape(NX, 2, NX, 8, HS)
        x = jnp.concatenate([x[:, :, FIRST_X:], x[:, :, :FIRST_X]], axis=2).reshape(NX, 8, 8, HS)
        return jnp.swapaxes(x, 0, 1).reshape(8, PAIRS, HS)

    for step in range(NY // 2):
        q = q_ref[:, 2 * step : 2 * step + 2].reshape(tile, HS)
        found = []
        for block, (keys_ref, values_ref) in enumerate(((own_ref, own_wide_ref), (got_ref, wide_ref))):
            keys = keys_ref[:SLOTS, :]
            scores = lax.dot_general(
                q, keys, (((1,), (1,)), ((), ())), preferred_element_type=jnp.float32
            )
            scores = scores + biases[block]
            peak = jnp.max(scores, axis=1, keepdims=True)
            weights = jnp.exp2((scores - peak) * EXP2_SCALE).astype(jnp.bfloat16)
            both = jnp.dot(weights, values_ref[...], preferred_element_type=jnp.float32)
            found.append((both[:, :HS], both[:, HS:], peak))
        (out0, sum0, peak0), (out1, sum1, peak1) = found
        ref = jnp.maximum(peak0, peak1).astype(jnp.bfloat16).astype(jnp.float32)
        scale0 = jnp.exp2((peak0 - ref) * EXP2_SCALE)
        scale1 = jnp.exp2((peak1 - ref) * EXP2_SCALE)
        out = by_slot(out0 * scale0 + out1 * scale1)
        total = sum0 * scale0 + sum1 * scale1
        high = total.astype(jnp.bfloat16).astype(jnp.float32)
        stats = jnp.where(part == 1, high, jnp.where(part == 2, total - high, resp))
        stats = jnp.where(part == 0, ref, stats)
        stats = jnp.where(diagonal, by_slot(stats), 0.0)
        stats = jnp.sum(stats, axis=1, keepdims=True)
        stats = jnp.where(sub == 0, stats, 0.0)
        full = jnp.concatenate([out, stats], axis=1).reshape(8 * SLOT_ROWS, HS)
        out_ref[8 * SLOT_ROWS * step : 8 * SLOT_ROWS * (step + 1), :] = full.astype(jnp.bfloat16)


def merge_kernel(parts_ref, out_ref):
    parts = parts_ref[...].astype(jnp.float32).reshape(SRC, SLOT_ROWS, HS)
    resp = parts[0, PAIRS : PAIRS + 1, 3 * PAIRS : 3 * PAIRS + 1].astype(jnp.int32)
    stats = parts[:, PAIRS, :]
    stats = jnp.concatenate([stats, jnp.zeros((HS - SRC, HS), jnp.float32)], axis=0).T
    valid = lane_ids((PAIRS, HS)) < SRC
    peaks = jnp.where(valid, stats[:PAIRS], -jnp.inf)
    sums = stats[PAIRS : 2 * PAIRS] + stats[2 * PAIRS : 3 * PAIRS]
    peak = jnp.max(peaks, axis=1, keepdims=True)
    scale = jnp.exp2((peaks - peak) * EXP2_SCALE)
    denom = jnp.sum(scale * sums, axis=1, keepdims=True)
    numer = parts[0, :PAIRS] * scale[:, 0:1]
    for src in range(1, SRC):
        numer = numer + parts[src, :PAIRS] * scale[:, src : src + 1]
    result = numer / denom
    rows = PAIRS // 8
    row = lax.broadcasted_iota(jnp.int32, (rows, HS), 0)
    live = row + rows * lax.axis_index(("z", "x", "core")) < resp
    for place in range(8):
        block = result[rows * place : rows * (place + 1)]
        head = (place + NC * FIRST_X) % 8
        out_ref[:, HS * head : HS * (head + 1)] = jnp.where(live, block, 0.0).astype(jnp.bfloat16)


VMEM = pl.BlockSpec(memory_space=pltpu.VMEM)
HBM = pl.BlockSpec(memory_space=pltpu.HBM)


def pack(queries, keys, values, counts, resp_len):
    return pl.pallas_call(
        pack_kernel,
        out_shape=(
            jax.ShapeDtypeStruct((NZ, NC, 16, HS), jnp.bfloat16),
            jax.ShapeDtypeStruct((SEND_ROWS, HS), jnp.bfloat16),
        ),
        in_specs=[VMEM] * 5,
        out_specs=(VMEM, VMEM),
        compiler_params=pltpu.CompilerParams(vmem_limit_bytes=60 * 2**20),
    )(queries, keys, values, counts.reshape(1, 1), resp_len.reshape(1, 1))


def widen(own, after):
    return pl.pallas_call(
        widen_kernel,
        out_shape=jax.ShapeDtypeStruct((SLOTS, 2 * HS), jnp.bfloat16),
        in_specs=[VMEM, HBM],
        out_specs=VMEM,
        compiler_params=pltpu.CompilerParams(vmem_limit_bytes=2**20),
    )(own, after)


def attend(spread, own, wide, got):
    return pl.pallas_call(
        attend_kernel,
        out_shape=jax.ShapeDtypeStruct((SRC * SLOT_ROWS, HS), jnp.bfloat16),
        in_specs=[VMEM, VMEM, VMEM, VMEM],
        out_specs=VMEM,
        scratch_shapes=[pltpu.VMEM((SLOTS, 2 * HS), jnp.bfloat16)],
        compiler_params=pltpu.CompilerParams(vmem_limit_bytes=12 * 2**20),
    )(spread, own, wide, got)


def merge(parts):
    return pl.pallas_call(
        merge_kernel,
        out_shape=jax.ShapeDtypeStruct((4, 8 * HS), jnp.bfloat16),
        in_specs=[VMEM],
        out_specs=VMEM,
        compiler_params=pltpu.CompilerParams(vmem_limit_bytes=4 * 2**20),
    )(parts)


def local(queries, keys, values, counts, resp_len):
    with jax.named_scope("query_spread"):
        slots, own = pack(queries, keys, values, counts, resp_len)
        halves = slots.reshape(NZ * NC, 16, HS)
        groups = exchange(halves, groups_zc()).reshape(NZ, PAIRS, HS)
    with jax.named_scope("pair_exchange"):
        got = lax.ppermute(own, "core", [(0, 1), (1, 0)])
    groups, own = lax.optimization_barrier((groups, own))
    with jax.named_scope("query_spread"):
        groups = jnp.broadcast_to(groups[None], (NX, NY, PAIRS, HS)).reshape(SRC, PAIRS, HS)
        spread = exchange(groups, groups_xy())
        spread = spread.reshape(NX, NY, PAIRS, HS)
    with jax.named_scope("attend"):
        wide = widen(own, spread)
        parts = attend(spread, own, wide, got)
    with jax.named_scope("merge"):
        parts = exchange(parts.reshape(SRC, SLOT_ROWS, HS), groups_zx())
        parts = parts.reshape(SRC * SLOT_ROWS, HS)
        return merge(parts)


def solution(mesh):
    grid = Mesh(mesh.devices.reshape(NZ, NX, NC, NY), ("z", "x", "core", "tp"))
    ctx = ("z", "x", "core")
    in_specs = (P("tp", ctx), P(ctx, "tp"), P(ctx, "tp"), P(ctx), P())
    return jax.shard_map(
        local, mesh=grid, in_specs=in_specs, out_specs=P(ctx, "tp"), check_vma=False
    )
```

```python
import jax
import jax.numpy as jnp
from jax import lax
from jax.experimental import pallas as pl
from jax.experimental.pallas import tpu as pltpu
from jax.sharding import Mesh, PartitionSpec as P

HS = 128
LOG2E = 1.4426950408889634
EXP2_SCALE = LOG2E / HS**0.5
NZ, NX, NC, NY = 8, 4, 2, 8
SLOTS = 1024
SRC = NZ * NX
PAIRS = 32
SLOT_ROWS = 40
SEND_ROWS = 2 * SLOTS + 16
COUNT_BASE = 64
FIRST_Z, FIRST_X, FIRST_Y, LAST_Z, LAST_X = 6, 2, 4, 4, 2
MASKED = -1e30


def lane_ids(shape):
    return lax.broadcasted_iota(jnp.int32, shape, len(shape) - 1)


def device(z, x, core, y):
    return ((z % NZ * NX + x % NX) * NC + core) * NY + y % NY


def groups_zc():
    return [
        [device(z + FIRST_Z, x, core, y) for z in range(NZ) for core in range(NC)]
        for x in range(NX)
        for y in range(NY)
    ]


def groups_xy():
    return [
        [device(z, x + FIRST_X, core, y + FIRST_Y) for x in range(NX) for y in range(NY)]
        for z in range(NZ)
        for core in range(NC)
    ]


def groups_zx():
    return [
        [device(z + LAST_Z, x + LAST_X, core, y) for z in range(NZ) for x in range(NX)]
        for core in range(NC)
        for y in range(NY)
    ]


def exchange(blocks, groups):
    axes = ("z", "x", "core", "tp")
    return lax.all_to_all(blocks, axes, 0, 0, axis_index_groups=groups, tiled=True)


def interleave(first, second):
    low = jnp.concatenate([first[:, :4], second[:, :4]], axis=1)
    high = jnp.concatenate([first[:, 4:], second[:, 4:]], axis=1)
    return low, high


def pack_kernel(query_ref, key_ref, value_ref, slots_ref, send_ref):
    rows = query_ref[...].astype(jnp.float32).reshape(2, 2, 8, HS)
    for core, half in enumerate(interleave(rows[:, 0], rows[:, 1])):
        half = half.reshape(16, HS).astype(jnp.bfloat16)
        for z in range(NZ):
            slots_ref[z, core] = half
    send_ref[:SLOTS, :] = key_ref[...]
    send_ref[SLOTS : 2 * SLOTS, :] = value_ref[...]
    send_ref[2 * SLOTS : SEND_ROWS, :] = jnp.zeros((16, HS), jnp.bfloat16)


def note_kernel(count_ref, resp_ref, _, send_ref, tail_ref, sem):
    count = count_ref[0]
    row = lax.broadcasted_iota(jnp.int32, (16, HS), 0)
    high = count // COUNT_BASE
    tail = jnp.where(row == 0, high, jnp.where(row == 1, count - high * COUNT_BASE, resp_ref[0]))
    tail_ref[...] = tail.astype(jnp.float32).astype(jnp.bfloat16)
    copy = pltpu.make_async_copy(tail_ref, send_ref.at[pl.ds(2 * SLOTS, 16)], sem)
    copy.start()
    copy.wait()


def widen_kernel(own_ref, _, wide_ref):
    wide_ref[:, :HS] = own_ref[SLOTS : 2 * SLOTS, :]
    wide_ref[:, HS:] = jnp.ones((SLOTS, HS), jnp.bfloat16)


def attend_kernel(q_ref, own_ref, own_wide_ref, got_ref, out_ref, wide_ref):
    wide_ref[:, :HS] = got_ref[SLOTS : 2 * SLOTS, :]
    wide_ref[:, HS:] = jnp.ones((SLOTS, HS), jnp.bfloat16)
    slot = lane_ids((1, SLOTS))
    biases = []
    for ref in (own_ref, got_ref):
        tail = ref[2 * SLOTS : SEND_ROWS, :].astype(jnp.float32)
        count = tail[0:1] * COUNT_BASE + tail[1:2]
        count = jnp.concatenate([count] * (SLOTS // HS), axis=1).astype(jnp.int32)
        biases.append(jnp.where(slot < count, 0.0, MASKED))
    resp = tail[2:3]

    tile = NX * PAIRS
    part = lane_ids((tile, HS)) // PAIRS
    pair = lax.broadcasted_iota(jnp.int32, (NX, PAIRS, HS), 1)
    lane = lane_ids((NX, PAIRS, HS))
    diagonal = lane % PAIRS == pair
    sub = lax.broadcasted_iota(jnp.int32, (NX, 8, HS), 1)

    def by_slot(x):
        x = x.reshape(NX, 2, 2, 8, HS)
        low, high = interleave(x[:, 0].reshape(-1, 8, HS), x[:, 1].reshape(-1, 8, HS))
        x = jnp.stack([low, high], axis=1).reshape(NX, NX, 8, HS)
        x = jnp.concatenate([x[:, LAST_X:], x[:, :LAST_X]], axis=1)
        return jnp.swapaxes(x, 0, 1).reshape(NX, PAIRS, HS)

    for step in range(NY):
        q = q_ref[:, step].reshape(tile, HS)
        found = []
        for block, (keys_ref, values_ref) in enumerate(((own_ref, own_wide_ref), (got_ref, wide_ref))):
            keys = keys_ref[:SLOTS, :]
            scores = lax.dot_general(
                q, keys, (((1,), (1,)), ((), ())), preferred_element_type=jnp.float32
            )
            scores = scores + biases[block]
            peak = jnp.max(scores, axis=1, keepdims=True)
            weights = jnp.exp2((scores - peak) * EXP2_SCALE).astype(jnp.bfloat16)
            both = jnp.dot(weights, values_ref[...], preferred_element_type=jnp.float32)
            found.append((both[:, :HS], both[:, HS:], peak))
        (out0, sum0, peak0), (out1, sum1, peak1) = found
        ref = jnp.maximum(peak0, peak1).astype(jnp.bfloat16).astype(jnp.float32)
        scale0 = jnp.exp2((peak0 - ref) * EXP2_SCALE)
        scale1 = jnp.exp2((peak1 - ref) * EXP2_SCALE)
        out = by_slot(out0 * scale0 + out1 * scale1)
        total = sum0 * scale0 + sum1 * scale1
        high = total.astype(jnp.bfloat16).astype(jnp.float32)
        stats = jnp.where(part == 1, high, jnp.where(part == 2, total - high, resp))
        stats = jnp.where(part == 0, ref, stats)
        stats = jnp.where(diagonal, by_slot(stats), 0.0)
        stats = jnp.sum(stats, axis=1, keepdims=True)
        stats = jnp.where(sub == 0, stats, 0.0)
        full = jnp.concatenate([out, stats], axis=1).reshape(NX * SLOT_ROWS, HS)
        place = (step + FIRST_Y - LAST_Z) % NZ * NX * SLOT_ROWS
        out_ref[place : place + NX * SLOT_ROWS, :] = full.astype(jnp.bfloat16)


def merge_kernel(parts_ref, out_ref):
    parts = parts_ref[...].astype(jnp.float32).reshape(SRC, SLOT_ROWS, HS)
    resp = parts[0, PAIRS : PAIRS + 1, 3 * PAIRS : 3 * PAIRS + 1].astype(jnp.int32)
    stats = parts[:, PAIRS, :]
    stats = jnp.concatenate([stats, jnp.zeros((HS - SRC, HS), jnp.float32)], axis=0).T
    valid = lane_ids((PAIRS, HS)) < SRC
    peaks = jnp.where(valid, stats[:PAIRS], -jnp.inf)
    sums = stats[PAIRS : 2 * PAIRS] + stats[2 * PAIRS : 3 * PAIRS]
    peak = jnp.max(peaks, axis=1, keepdims=True)
    scale = jnp.exp2((peaks - peak) * EXP2_SCALE)
    denom = jnp.sum(scale * sums, axis=1, keepdims=True)
    numer = parts[0, :PAIRS] * scale[:, 0:1]
    for src in range(1, SRC):
        numer = numer + parts[src, :PAIRS] * scale[:, src : src + 1]
    result = numer / denom
    rows = PAIRS // 8
    row = lax.broadcasted_iota(jnp.int32, (rows, HS), 0)
    live = row + rows * lax.axis_index(("z", "x", "core")) < resp
    for place in range(8):
        block = result[rows * place : rows * (place + 1)]
        head = (place + NC * FIRST_X) % 8
        out_ref[:, HS * head : HS * (head + 1)] = jnp.where(live, block, 0.0).astype(jnp.bfloat16)


VMEM = pl.BlockSpec(memory_space=pltpu.VMEM)
SMEM = pl.BlockSpec(memory_space=pltpu.SMEM)
HBM = pl.BlockSpec(memory_space=pltpu.HBM)


def pack(queries, keys, values):
    return pl.pallas_call(
        pack_kernel,
        out_shape=(
            jax.ShapeDtypeStruct((NZ, NC, 16, HS), jnp.bfloat16),
            jax.ShapeDtypeStruct((SEND_ROWS, HS), jnp.bfloat16),
        ),
        in_specs=[VMEM] * 3,
        out_specs=(VMEM, VMEM),
        compiler_params=pltpu.CompilerParams(vmem_limit_bytes=60 * 2**20),
    )(queries, keys, values)


def note(counts, resp_len, own):
    return pl.pallas_call(
        note_kernel,
        out_shape=jax.ShapeDtypeStruct((SEND_ROWS, HS), jnp.bfloat16),
        in_specs=[SMEM, SMEM, HBM],
        out_specs=HBM,
        input_output_aliases={2: 0},
        scratch_shapes=[pltpu.VMEM((16, HS), jnp.bfloat16), pltpu.SemaphoreType.DMA],
        compiler_params=pltpu.CompilerParams(vmem_limit_bytes=60 * 2**20),
    )(counts, resp_len, own)


def widen(own, after):
    return pl.pallas_call(
        widen_kernel,
        out_shape=jax.ShapeDtypeStruct((SLOTS, 2 * HS), jnp.bfloat16),
        in_specs=[VMEM, HBM],
        out_specs=VMEM,
        compiler_params=pltpu.CompilerParams(vmem_limit_bytes=2**20),
    )(own, after)


def attend(spread, own, wide, got):
    return pl.pallas_call(
        attend_kernel,
        out_shape=jax.ShapeDtypeStruct((SRC * SLOT_ROWS, HS), jnp.bfloat16),
        in_specs=[VMEM, VMEM, VMEM, VMEM],
        out_specs=VMEM,
        scratch_shapes=[pltpu.VMEM((SLOTS, 2 * HS), jnp.bfloat16)],
        compiler_params=pltpu.CompilerParams(vmem_limit_bytes=12 * 2**20),
    )(spread, own, wide, got)


def merge(parts):
    return pl.pallas_call(
        merge_kernel,
        out_shape=jax.ShapeDtypeStruct((4, 8 * HS), jnp.bfloat16),
        in_specs=[VMEM],
        out_specs=VMEM,
        compiler_params=pltpu.CompilerParams(vmem_limit_bytes=4 * 2**20),
    )(parts)


def local(queries, keys, values, counts, resp_len):
    with jax.named_scope("query_spread"):
        slots, own = pack(queries, keys, values)
        halves = slots.reshape(NZ * NC, 16, HS)
        groups = exchange(halves, groups_zc()).reshape(NZ, PAIRS, HS)
    with jax.named_scope("pair_exchange"):
        own = note(counts, resp_len, own)
        got = lax.ppermute(own, "core", [(0, 1), (1, 0)])
    groups, own = lax.optimization_barrier((groups, own))
    with jax.named_scope("query_spread"):
        groups = jnp.roll(groups, FIRST_Z - FIRST_Y, axis=0)
        groups = jnp.broadcast_to(groups[None], (NX, NY, PAIRS, HS)).reshape(SRC, PAIRS, HS)
        spread = exchange(groups, groups_xy())
        spread = spread.reshape(NX, NY, PAIRS, HS)
    with jax.named_scope("attend"):
        wide = widen(own, spread)
        parts = attend(spread, own, wide, got)
    with jax.named_scope("merge"):
        parts = exchange(parts.reshape(SRC, SLOT_ROWS, HS), groups_zx())
        parts = parts.reshape(SRC * SLOT_ROWS, HS)
        return merge(parts)


def solution(mesh):
    grid = Mesh(mesh.devices.reshape(NZ, NX, NC, NY), ("z", "x", "core", "tp"))
    ctx = ("z", "x", "core")
    in_specs = (P("tp", ctx), P(ctx, "tp"), P(ctx, "tp"), P(ctx), P())
    return jax.shard_map(
        local, mesh=grid, in_specs=in_specs, out_specs=P(ctx, "tp"), check_vma=False
    )
```

```python
import jax
import jax.numpy as jnp
from jax import lax
from jax.experimental import pallas as pl
from jax.experimental.pallas import tpu as pltpu
from jax.sharding import Mesh, PartitionSpec as P

HS = 128
LOG2E = 1.4426950408889634
EXP2_SCALE = LOG2E / HS**0.5
NZ, NX, NC, NY = 8, 4, 2, 8
SLOTS = 1024
SRC = NZ * NX
PAIRS = 32
SLOT_ROWS = 40
SEND_ROWS = 2 * SLOTS + 16
COUNT_BASE = 64
FIRST_Z, FIRST_X, FIRST_Y, LAST_Z, LAST_X = 6, 3, 4, 4, 2
MASKED = -1e30


def lane_ids(shape):
    return lax.broadcasted_iota(jnp.int32, shape, len(shape) - 1)


def device(z, x, core, y):
    return ((z % NZ * NX + x % NX) * NC + core) * NY + y % NY


def groups_zc():
    return [
        [device(z + FIRST_Z, x, core, y) for z in range(NZ) for core in range(NC)]
        for x in range(NX)
        for y in range(NY)
    ]


def groups_xy():
    return [
        [device(z, x + FIRST_X, core, y + FIRST_Y) for x in range(NX) for y in range(NY)]
        for z in range(NZ)
        for core in range(NC)
    ]


def groups_zx():
    return [
        [device(z + LAST_Z, x + LAST_X, core, y) for z in range(NZ) for x in range(NX)]
        for core in range(NC)
        for y in range(NY)
    ]


def exchange(blocks, groups):
    axes = ("z", "x", "core", "tp")
    return lax.all_to_all(blocks, axes, 0, 0, axis_index_groups=groups, tiled=True)


def interleave(first, second):
    low = jnp.concatenate([first[:, :4], second[:, :4]], axis=1)
    high = jnp.concatenate([first[:, 4:], second[:, 4:]], axis=1)
    return low, high


def pack_kernel(query_ref, key_ref, value_ref, slots_ref, send_ref, rows, slots, both, sems):
    def copy(source, target, which):
        made = pltpu.make_async_copy(source, target, sems.at[which])
        made.start()
        return made

    first, second = pl.ds(0, SLOTS), pl.ds(SLOTS, SLOTS)
    loads = (
        copy(query_ref, rows, 0),
        copy(key_ref, both.at[first], 1),
        copy(value_ref, both.at[second], 2),
    )
    loads[0].wait()
    halves = rows[...].astype(jnp.float32).reshape(2, 2, 8, HS)
    for core, half in enumerate(interleave(halves[:, 0], halves[:, 1])):
        half = half.reshape(16, HS).astype(jnp.bfloat16)
        for z in range(NZ):
            slots[z, core] = half
    stores = [copy(slots, slots_ref, 3)]
    for which, part in enumerate((first, second)):
        loads[1 + which].wait()
        stores.append(copy(both.at[part], send_ref.at[part], 4 + which))
    for store in stores:
        store.wait()


def note_kernel(count_ref, resp_ref, _, send_ref, tail_ref, sem):
    count = count_ref[0]
    row = lax.broadcasted_iota(jnp.int32, (16, HS), 0)
    high = count // COUNT_BASE
    tail = jnp.where(row == 0, high, jnp.where(row == 1, count - high * COUNT_BASE, resp_ref[0]))
    tail_ref[...] = tail.astype(jnp.float32).astype(jnp.bfloat16)
    copy = pltpu.make_async_copy(tail_ref, send_ref.at[pl.ds(2 * SLOTS, 16)], sem)
    copy.start()
    copy.wait()


def widen_kernel(own_ref, _, wide_ref):
    wide_ref[:, :HS] = own_ref[SLOTS : 2 * SLOTS, :]
    wide_ref[:, HS:] = jnp.ones((SLOTS, HS), jnp.bfloat16)


def attend_kernel(q_ref, own_ref, own_wide_ref, got_ref, out_ref, wide_ref):
    wide_ref[:, :HS] = got_ref[SLOTS : 2 * SLOTS, :]
    wide_ref[:, HS:] = jnp.ones((SLOTS, HS), jnp.bfloat16)
    slot = lane_ids((1, SLOTS))
    biases = []
    for ref in (own_ref, got_ref):
        tail = ref[2 * SLOTS : SEND_ROWS, :].astype(jnp.float32)
        count = tail[0:1] * COUNT_BASE + tail[1:2]
        count = jnp.concatenate([count] * (SLOTS // HS), axis=1).astype(jnp.int32)
        biases.append(jnp.where(slot < count, 0.0, MASKED))
    resp = tail[2:3]

    tile = NX * PAIRS
    part = lane_ids((tile, HS)) // PAIRS
    pair = lax.broadcasted_iota(jnp.int32, (NX, PAIRS, HS), 1)
    lane = lane_ids((NX, PAIRS, HS))
    diagonal = lane % PAIRS == pair
    sub = lax.broadcasted_iota(jnp.int32, (NX, 8, HS), 1)

    def by_slot(x):
        x = x.reshape(NX, 2, 2, 8, HS)
        low, high = interleave(x[:, 0].reshape(-1, 8, HS), x[:, 1].reshape(-1, 8, HS))
        x = jnp.stack([low, high], axis=1).reshape(NX, NX, 8, HS)
        x = jnp.concatenate([x[:, LAST_X:], x[:, :LAST_X]], axis=1)
        return jnp.swapaxes(x, 0, 1).reshape(NX, PAIRS, HS)

    for step in range(NY):
        q = q_ref[:, step].reshape(tile, HS)
        found = []
        for block, (keys_ref, values_ref) in enumerate(((own_ref, own_wide_ref), (got_ref, wide_ref))):
            keys = keys_ref[:SLOTS, :]
            scores = lax.dot_general(
                q, keys, (((1,), (1,)), ((), ())), preferred_element_type=jnp.float32
            )
            scores = scores + biases[block]
            peak = jnp.max(scores, axis=1, keepdims=True)
            weights = jnp.exp2((scores - peak) * EXP2_SCALE).astype(jnp.bfloat16)
            both = jnp.dot(weights, values_ref[...], preferred_element_type=jnp.float32)
            found.append((both[:, :HS], both[:, HS:], peak))
        (out0, sum0, peak0), (out1, sum1, peak1) = found
        ref = jnp.maximum(peak0, peak1).astype(jnp.bfloat16).astype(jnp.float32)
        scale0 = jnp.exp2((peak0 - ref) * EXP2_SCALE)
        scale1 = jnp.exp2((peak1 - ref) * EXP2_SCALE)
        out = by_slot(out0 * scale0 + out1 * scale1)
        total = sum0 * scale0 + sum1 * scale1
        high = total.astype(jnp.bfloat16).astype(jnp.float32)
        stats = jnp.where(part == 1, high, jnp.where(part == 2, total - high, resp))
        stats = jnp.where(part == 0, ref, stats)
        stats = jnp.where(diagonal, by_slot(stats), 0.0)
        stats = jnp.sum(stats, axis=1, keepdims=True)
        stats = jnp.where(sub == 0, stats, 0.0)
        full = jnp.concatenate([out, stats], axis=1).reshape(NX * SLOT_ROWS, HS)
        place = (step + FIRST_Y - LAST_Z) % NZ * NX * SLOT_ROWS
        out_ref[place : place + NX * SLOT_ROWS, :] = full.astype(jnp.bfloat16)


def merge_kernel(parts_ref, out_ref):
    parts = parts_ref[...].astype(jnp.float32).reshape(SRC, SLOT_ROWS, HS)
    resp = parts[0, PAIRS : PAIRS + 1, 3 * PAIRS : 3 * PAIRS + 1].astype(jnp.int32)
    stats = parts[:, PAIRS, :]
    stats = jnp.concatenate([stats, jnp.zeros((HS - SRC, HS), jnp.float32)], axis=0).T
    valid = lane_ids((PAIRS, HS)) < SRC
    peaks = jnp.where(valid, stats[:PAIRS], -jnp.inf)
    sums = stats[PAIRS : 2 * PAIRS] + stats[2 * PAIRS : 3 * PAIRS]
    peak = jnp.max(peaks, axis=1, keepdims=True)
    scale = jnp.exp2((peaks - peak) * EXP2_SCALE)
    denom = jnp.sum(scale * sums, axis=1, keepdims=True)
    numer = parts[0, :PAIRS] * scale[:, 0:1]
    for src in range(1, SRC):
        numer = numer + parts[src, :PAIRS] * scale[:, src : src + 1]
    result = numer / denom
    rows = PAIRS // 8
    row = lax.broadcasted_iota(jnp.int32, (rows, HS), 0)
    live = row + rows * lax.axis_index(("z", "x", "core")) < resp
    for place in range(8):
        block = result[rows * place : rows * (place + 1)]
        head = (place + NC * FIRST_X) % 8
        out_ref[:, HS * head : HS * (head + 1)] = jnp.where(live, block, 0.0).astype(jnp.bfloat16)


VMEM = pl.BlockSpec(memory_space=pltpu.VMEM)
SMEM = pl.BlockSpec(memory_space=pltpu.SMEM)
HBM = pl.BlockSpec(memory_space=pltpu.HBM)


def pack(queries, keys, values):
    return pl.pallas_call(
        pack_kernel,
        out_shape=(
            jax.ShapeDtypeStruct((NZ, NC, 16, HS), jnp.bfloat16),
            jax.ShapeDtypeStruct((SEND_ROWS, HS), jnp.bfloat16),
        ),
        in_specs=[HBM] * 3,
        out_specs=(HBM, HBM),
        scratch_shapes=[
            pltpu.VMEM((PAIRS, HS), jnp.bfloat16),
            pltpu.VMEM((NZ, NC, 16, HS), jnp.bfloat16),
            pltpu.VMEM((2 * SLOTS, HS), jnp.bfloat16),
            pltpu.SemaphoreType.DMA((6,)),
        ],
        compiler_params=pltpu.CompilerParams(vmem_limit_bytes=60 * 2**20),
    )(queries, keys, values)


def note(counts, resp_len, own):
    return pl.pallas_call(
        note_kernel,
        out_shape=jax.ShapeDtypeStruct((SEND_ROWS, HS), jnp.bfloat16),
        in_specs=[SMEM, SMEM, HBM],
        out_specs=HBM,
        input_output_aliases={2: 0},
        scratch_shapes=[pltpu.VMEM((16, HS), jnp.bfloat16), pltpu.SemaphoreType.DMA],
        compiler_params=pltpu.CompilerParams(vmem_limit_bytes=60 * 2**20),
    )(counts, resp_len, own)


def widen(own, after):
    return pl.pallas_call(
        widen_kernel,
        out_shape=jax.ShapeDtypeStruct((SLOTS, 2 * HS), jnp.bfloat16),
        in_specs=[VMEM, HBM],
        out_specs=VMEM,
        compiler_params=pltpu.CompilerParams(vmem_limit_bytes=2**20),
    )(own, after)


def attend(spread, own, wide, got):
    return pl.pallas_call(
        attend_kernel,
        out_shape=jax.ShapeDtypeStruct((SRC * SLOT_ROWS, HS), jnp.bfloat16),
        in_specs=[VMEM, VMEM, VMEM, VMEM],
        out_specs=VMEM,
        scratch_shapes=[pltpu.VMEM((SLOTS, 2 * HS), jnp.bfloat16)],
        compiler_params=pltpu.CompilerParams(vmem_limit_bytes=12 * 2**20),
    )(spread, own, wide, got)


def merge(parts):
    return pl.pallas_call(
        merge_kernel,
        out_shape=jax.ShapeDtypeStruct((4, 8 * HS), jnp.bfloat16),
        in_specs=[VMEM],
        out_specs=VMEM,
        compiler_params=pltpu.CompilerParams(vmem_limit_bytes=4 * 2**20),
    )(parts)


def local(queries, keys, values, counts, resp_len):
    with jax.named_scope("query_spread"):
        slots, own = pack(queries, keys, values)
        halves = slots.reshape(NZ * NC, 16, HS)
        groups = exchange(halves, groups_zc()).reshape(NZ, PAIRS, HS)
    with jax.named_scope("pair_exchange"):
        own = note(counts, resp_len, own)
        got = lax.ppermute(own, "core", [(0, 1), (1, 0)])
    groups, own = lax.optimization_barrier((groups, own))
    with jax.named_scope("query_spread"):
        groups = jnp.roll(groups, FIRST_Z - FIRST_Y, axis=0)
        groups = jnp.broadcast_to(groups[None], (NX, NY, PAIRS, HS)).reshape(SRC, PAIRS, HS)
        spread = exchange(groups, groups_xy())
        spread = spread.reshape(NX, NY, PAIRS, HS)
    with jax.named_scope("attend"):
        wide = widen(own, spread)
        parts = attend(spread, own, wide, got)
    with jax.named_scope("merge"):
        parts = exchange(parts.reshape(SRC, SLOT_ROWS, HS), groups_zx())
        parts = parts.reshape(SRC * SLOT_ROWS, HS)
        return merge(parts)


def solution(mesh):
    grid = Mesh(mesh.devices.reshape(NZ, NX, NC, NY), ("z", "x", "core", "tp"))
    ctx = ("z", "x", "core")
    in_specs = (P("tp", ctx), P(ctx, "tp"), P(ctx, "tp"), P(ctx), P())
    return jax.shard_map(
        local, mesh=grid, in_specs=in_specs, out_specs=P(ctx, "tp"), check_vma=False
    )
```

```python
import jax
import jax.numpy as jnp
from jax import lax
from jax.experimental import pallas as pl
from jax.experimental.pallas import tpu as pltpu
from jax.sharding import Mesh, PartitionSpec as P

HS = 128
LOG2E = 1.4426950408889634
EXP2_SCALE = LOG2E / HS**0.5
NZ, NX, NC, NY = 8, 4, 2, 8
SLOTS = 1024
SRC = NZ * NX
PAIRS = 32
SLOT_ROWS = 40
SEND_ROWS = 2 * SLOTS + 16
COUNT_BASE = 64
FIRST_Z, FIRST_X, FIRST_Y, LAST_Z, LAST_X = 6, 3, 4, 4, 2
MASKED = -1e30


def lane_ids(shape):
    return lax.broadcasted_iota(jnp.int32, shape, len(shape) - 1)


def device(z, x, core, y):
    return ((z % NZ * NX + x % NX) * NC + core) * NY + y % NY


def groups_zc():
    return [
        [device(z + FIRST_Z, x, core, y) for z in range(NZ) for core in range(NC)]
        for x in range(NX)
        for y in range(NY)
    ]


def groups_xy():
    return [
        [device(z, x + FIRST_X, core, y + FIRST_Y) for x in range(NX) for y in range(NY)]
        for z in range(NZ)
        for core in range(NC)
    ]


def groups_zx():
    return [
        [device(z + LAST_Z, x + LAST_X, core, y) for z in range(NZ) for x in range(NX)]
        for core in range(NC)
        for y in range(NY)
    ]


def exchange(blocks, groups):
    axes = ("z", "x", "core", "tp")
    return lax.all_to_all(blocks, axes, 0, 0, axis_index_groups=groups, tiled=True)


def interleave(first, second):
    low = jnp.concatenate([first[:, :4], second[:, :4]], axis=1)
    high = jnp.concatenate([first[:, 4:], second[:, 4:]], axis=1)
    return low, high


def halves_kernel(query_ref, slots_ref):
    rows = query_ref[...].astype(jnp.float32).reshape(2, 2, 8, HS)
    for core, half in enumerate(interleave(rows[:, 0], rows[:, 1])):
        half = half.reshape(16, HS).astype(jnp.bfloat16)
        for z in range(NZ):
            slots_ref[z, core] = half


def pack_kernel(count_ref, resp_ref, key_ref, value_ref, _, send_ref, sems):
    copies = [
        pltpu.make_async_copy(key_ref, send_ref.at[pl.ds(0, SLOTS)], sems.at[0]),
        pltpu.make_async_copy(value_ref, send_ref.at[pl.ds(SLOTS, SLOTS)], sems.at[1]),
    ]
    for copy in copies:
        copy.start()
    count = count_ref[0]
    high = count // COUNT_BASE
    row = lax.broadcasted_iota(jnp.int32, (16, HS), 0)
    tail = jnp.where(row == 0, high, jnp.where(row == 1, count - high * COUNT_BASE, resp_ref[0]))
    send_ref[2 * SLOTS : SEND_ROWS, :] = tail.astype(jnp.float32).astype(jnp.bfloat16)
    for copy in copies:
        copy.wait()


def widen_kernel(own_ref, _, wide_ref):
    wide_ref[:, :HS] = own_ref[SLOTS : 2 * SLOTS, :]
    wide_ref[:, HS:] = jnp.ones((SLOTS, HS), jnp.bfloat16)


def attend_kernel(q_ref, own_ref, own_wide_ref, got_ref, out_ref, wide_ref):
    wide_ref[:, :HS] = got_ref[SLOTS : 2 * SLOTS, :]
    wide_ref[:, HS:] = jnp.ones((SLOTS, HS), jnp.bfloat16)
    slot = lane_ids((1, SLOTS))
    biases = []
    for ref in (own_ref, got_ref):
        tail = ref[2 * SLOTS : SEND_ROWS, :].astype(jnp.float32)
        count = tail[0:1] * COUNT_BASE + tail[1:2]
        count = jnp.concatenate([count] * (SLOTS // HS), axis=1).astype(jnp.int32)
        biases.append(jnp.where(slot < count, 0.0, MASKED))
    resp = tail[2:3]

    tile = NX * PAIRS
    part = lane_ids((tile, HS)) // PAIRS
    pair = lax.broadcasted_iota(jnp.int32, (NX, PAIRS, HS), 1)
    lane = lane_ids((NX, PAIRS, HS))
    diagonal = lane % PAIRS == pair
    sub = lax.broadcasted_iota(jnp.int32, (NX, 8, HS), 1)

    def by_slot(x):
        x = x.reshape(NX, 2, 2, 8, HS)
        low, high = interleave(x[:, 0].reshape(-1, 8, HS), x[:, 1].reshape(-1, 8, HS))
        x = jnp.stack([low, high], axis=1).reshape(NX, NX, 8, HS)
        x = jnp.concatenate([x[:, LAST_X:], x[:, :LAST_X]], axis=1)
        return jnp.swapaxes(x, 0, 1).reshape(NX, PAIRS, HS)

    for step in range(NY):
        q = q_ref[:, step].reshape(tile, HS)
        found = []
        for block, (keys_ref, values_ref) in enumerate(((own_ref, own_wide_ref), (got_ref, wide_ref))):
            keys = keys_ref[:SLOTS, :]
            scores = lax.dot_general(
                q, keys, (((1,), (1,)), ((), ())), preferred_element_type=jnp.float32
            )
            scores = scores + biases[block]
            peak = jnp.max(scores, axis=1, keepdims=True)
            weights = jnp.exp2((scores - peak) * EXP2_SCALE).astype(jnp.bfloat16)
            both = jnp.dot(weights, values_ref[...], preferred_element_type=jnp.float32)
            found.append((both[:, :HS], both[:, HS:], peak))
        (out0, sum0, peak0), (out1, sum1, peak1) = found
        ref = jnp.maximum(peak0, peak1).astype(jnp.bfloat16).astype(jnp.float32)
        scale0 = jnp.exp2((peak0 - ref) * EXP2_SCALE)
        scale1 = jnp.exp2((peak1 - ref) * EXP2_SCALE)
        out = by_slot(out0 * scale0 + out1 * scale1)
        total = sum0 * scale0 + sum1 * scale1
        high = total.astype(jnp.bfloat16).astype(jnp.float32)
        stats = jnp.where(part == 1, high, jnp.where(part == 2, total - high, resp))
        stats = jnp.where(part == 0, ref, stats)
        stats = jnp.where(diagonal, by_slot(stats), 0.0)
        stats = jnp.sum(stats, axis=1, keepdims=True)
        stats = jnp.where(sub == 0, stats, 0.0)
        full = jnp.concatenate([out, stats], axis=1).reshape(NX * SLOT_ROWS, HS)
        place = (step + FIRST_Y - LAST_Z) % NZ * NX * SLOT_ROWS
        out_ref[place : place + NX * SLOT_ROWS, :] = full.astype(jnp.bfloat16)


def merge_kernel(parts_ref, out_ref):
    parts = parts_ref[...].astype(jnp.float32).reshape(SRC, SLOT_ROWS, HS)
    resp = parts[0, PAIRS : PAIRS + 1, 3 * PAIRS : 3 * PAIRS + 1].astype(jnp.int32)
    stats = parts[:, PAIRS, :]
    stats = jnp.concatenate([stats, jnp.zeros((HS - SRC, HS), jnp.float32)], axis=0).T
    valid = lane_ids((PAIRS, HS)) < SRC
    peaks = jnp.where(valid, stats[:PAIRS], -jnp.inf)
    sums = stats[PAIRS : 2 * PAIRS] + stats[2 * PAIRS : 3 * PAIRS]
    peak = jnp.max(peaks, axis=1, keepdims=True)
    scale = jnp.exp2((peaks - peak) * EXP2_SCALE)
    denom = jnp.sum(scale * sums, axis=1, keepdims=True)
    numer = parts[0, :PAIRS] * scale[:, 0:1]
    for src in range(1, SRC):
        numer = numer + parts[src, :PAIRS] * scale[:, src : src + 1]
    result = numer / denom
    rows = PAIRS // 8
    row = lax.broadcasted_iota(jnp.int32, (rows, HS), 0)
    live = row + rows * lax.axis_index(("z", "x", "core")) < resp
    for place in range(8):
        block = result[rows * place : rows * (place + 1)]
        head = (place + NC * FIRST_X) % 8
        out_ref[:, HS * head : HS * (head + 1)] = jnp.where(live, block, 0.0).astype(jnp.bfloat16)


VMEM = pl.BlockSpec(memory_space=pltpu.VMEM)
SMEM = pl.BlockSpec(memory_space=pltpu.SMEM)
HBM = pl.BlockSpec(memory_space=pltpu.HBM)


def split_halves(queries):
    return pl.pallas_call(
        halves_kernel,
        out_shape=jax.ShapeDtypeStruct((NZ, NC, 16, HS), jnp.bfloat16),
        in_specs=[VMEM],
        out_specs=VMEM,
        compiler_params=pltpu.CompilerParams(vmem_limit_bytes=2**20),
    )(queries)


def pack(counts, resp_len, keys, values, after):
    return pl.pallas_call(
        pack_kernel,
        out_shape=jax.ShapeDtypeStruct((SEND_ROWS, HS), jnp.bfloat16),
        in_specs=[SMEM, SMEM, HBM, HBM, HBM],
        out_specs=VMEM,
        scratch_shapes=[pltpu.SemaphoreType.DMA((2,))],
        compiler_params=pltpu.CompilerParams(vmem_limit_bytes=2 * 2**20),
        cost_estimate=pl.CostEstimate(flops=0, bytes_accessed=2**23, transcendentals=0),
    )(counts, resp_len, keys, values, after)


def widen(own, after):
    return pl.pallas_call(
        widen_kernel,
        out_shape=jax.ShapeDtypeStruct((SLOTS, 2 * HS), jnp.bfloat16),
        in_specs=[VMEM, HBM],
        out_specs=VMEM,
        compiler_params=pltpu.CompilerParams(vmem_limit_bytes=2**20),
        cost_estimate=pl.CostEstimate(flops=2**33, bytes_accessed=2**21, transcendentals=0),
    )(own, after)


def attend(spread, own, wide, got):
    return pl.pallas_call(
        attend_kernel,
        out_shape=jax.ShapeDtypeStruct((SRC * SLOT_ROWS, HS), jnp.bfloat16),
        in_specs=[VMEM, VMEM, VMEM, VMEM],
        out_specs=VMEM,
        scratch_shapes=[pltpu.VMEM((SLOTS, 2 * HS), jnp.bfloat16)],
        compiler_params=pltpu.CompilerParams(vmem_limit_bytes=12 * 2**20),
    )(spread, own, wide, got)


def merge(parts):
    return pl.pallas_call(
        merge_kernel,
        out_shape=jax.ShapeDtypeStruct((4, 8 * HS), jnp.bfloat16),
        in_specs=[VMEM],
        out_specs=VMEM,
        compiler_params=pltpu.CompilerParams(vmem_limit_bytes=4 * 2**20),
    )(parts)


def local(queries, keys, values, counts, resp_len):
    with jax.named_scope("query_spread"):
        halves = split_halves(queries).reshape(NZ * NC, 16, HS)
        groups = exchange(halves, groups_zc()).reshape(NZ, PAIRS, HS)
        groups = jnp.roll(groups, FIRST_Z - FIRST_Y, axis=0)
        groups = jnp.broadcast_to(groups[None], (NX, NY, PAIRS, HS)).reshape(SRC, PAIRS, HS)
        spread = exchange(groups, groups_xy()).reshape(NX, NY, PAIRS, HS)
    with jax.named_scope("pair_exchange"):
        own = pack(counts, resp_len, keys, values, groups)
        got = lax.ppermute(own, "core", [(0, 1), (1, 0)])
    with jax.named_scope("attend"):
        wide = widen(own, spread)
        parts = attend(spread, own, wide, got)
    with jax.named_scope("merge"):
        parts = exchange(parts.reshape(SRC, SLOT_ROWS, HS), groups_zx())
        parts = parts.reshape(SRC * SLOT_ROWS, HS)
        return merge(parts)


def solution(mesh):
    grid = Mesh(mesh.devices.reshape(NZ, NX, NC, NY), ("z", "x", "core", "tp"))
    ctx = ("z", "x", "core")
    in_specs = (P("tp", ctx), P(ctx, "tp"), P(ctx, "tp"), P(ctx), P())
    return jax.shard_map(
        local, mesh=grid, in_specs=in_specs, out_specs=P(ctx, "tp"), check_vma=False
    )
```

```python
import jax
import jax.numpy as jnp
from jax import lax
from jax.experimental import pallas as pl
from jax.experimental.pallas import tpu as pltpu
from jax.sharding import Mesh, PartitionSpec as P

HS = 128
LOG2E = 1.4426950408889634
EXP2_SCALE = LOG2E / HS**0.5
NZ, NX, NC, NY = 8, 4, 2, 8
SLOTS = 1024
TILE = 128
TILES = 4
PAIRS = 32
SLOT_ROWS = 40
SRC = NZ * 2
SEND_ROWS = 2 * SLOTS + 16
COUNT_BASE = 64
MASKED = -1e30
FIRST_Z, FIRST_Y, LAST_Z = 6, 4, 4
SHARERS = ((0, 1), (3, 2))
CLASSES = ((3, 0), (2, 1))
HEAD_X = (3, 2, 0, 1)


def lane_ids(shape):
    return lax.broadcasted_iota(jnp.int32, shape, len(shape) - 1)


def device(z, x, core, y):
    return ((z % NZ * NX + x % NX) * NC + core) * NY + y % NY


def groups_spread():
    return [
        [device(z + FIRST_Z, x, core, y) for z in range(NZ) for x in pair for core in range(NC)]
        for pair in SHARERS
        for y in range(NY)
    ]


def groups_turn():
    return [
        [device(z, x, core, y + FIRST_Y) for x in pair for y in range(NY)]
        for z in range(NZ)
        for core in range(NC)
        for pair in CLASSES
    ]


def groups_merge():
    return [
        [device(z + LAST_Z, x, core, y) for z in range(NZ) for x in pair]
        for core in range(NC)
        for y in range(NY)
        for pair in CLASSES
    ]


def exchange(blocks, groups):
    axes = ("z", "x", "core", "tp")
    return lax.all_to_all(blocks, axes, 0, 0, axis_index_groups=groups, tiled=True)


def interleave(first, second):
    low = jnp.concatenate([first[:, :4], second[:, :4]], axis=1)
    high = jnp.concatenate([first[:, 4:], second[:, 4:]], axis=1)
    return low, high


def slots_kernel(query_ref, slots_ref):
    by_x = query_ref[...].astype(jnp.float32).reshape(NX, 8, HS)
    parts = []
    for upper, lower in CLASSES:
        parts += interleave(by_x[upper : upper + 1], by_x[lower : lower + 1])
    block = jnp.concatenate(parts, axis=0).reshape(PAIRS, HS).astype(jnp.bfloat16)
    for z in range(NZ):
        slots_ref[z] = block


def pack_kernel(count_ref, resp_ref, key_ref, value_ref, _, send_ref, sems):
    copies = [
        pltpu.make_async_copy(key_ref, send_ref.at[pl.ds(0, SLOTS)], sems.at[0]),
        pltpu.make_async_copy(value_ref, send_ref.at[pl.ds(SLOTS, SLOTS)], sems.at[1]),
    ]
    for copy in copies:
        copy.start()
    count = count_ref[0]
    high = count // COUNT_BASE
    row = lax.broadcasted_iota(jnp.int32, (16, HS), 0)
    tail = jnp.where(row == 0, high, jnp.where(row == 1, count - high * COUNT_BASE, resp_ref[0]))
    send_ref[2 * SLOTS : SEND_ROWS, :] = tail.astype(jnp.float32).astype(jnp.bfloat16)
    for copy in copies:
        copy.wait()


def turn_kernel(groups_ref, turned_ref):
    for place in range(NY):
        block = groups_ref[(place + FIRST_Y - FIRST_Z) % NZ]
        for x in range(2):
            turned_ref[x, place] = block


def widen_into(wide_ref, ref):
    wide_ref[:, :HS] = ref[SLOTS : 2 * SLOTS, :]
    wide_ref[:, HS:] = jnp.ones((SLOTS, HS), jnp.bfloat16)


def tail_rows(ref):
    return ref[2 * SLOTS : SEND_ROWS, :].astype(jnp.float32)


def bias_row(ref):
    tail = tail_rows(ref)
    count = tail[0:1] * COUNT_BASE + tail[1:2]
    count = jnp.concatenate([count] * (SLOTS // HS), axis=1).astype(jnp.int32)
    return jnp.where(lane_ids((1, SLOTS)) < count, 0.0, MASKED)


def one_block(q, ref, wide_ref, bias):
    scores = lax.dot_general(
        q, ref[:SLOTS, :], (((1,), (1,)), ((), ())), preferred_element_type=jnp.float32
    )
    scores = scores + bias
    peak = jnp.max(scores, axis=1, keepdims=True)
    weights = jnp.exp2((scores - peak) * EXP2_SCALE).astype(jnp.bfloat16)
    both = jnp.dot(weights, wide_ref[...], preferred_element_type=jnp.float32)
    return both[:, :HS], both[:, HS:], jnp.broadcast_to(peak, (TILE, HS))


def combine(found, ref):
    out, total = 0.0, 0.0
    for block_out, block_sum, peak in found:
        scale = jnp.exp2((peak - ref) * EXP2_SCALE)
        out = out + block_out * scale
        total = total + block_sum * scale
    return out, total


def query_tile(q_ref, step):
    return q_ref[:, 2 * step : 2 * step + 2].reshape(TILE, HS)


def attend_kernel(q_ref, own_ref, near_ref, out_ref, own_wide_ref, near_wide_ref):
    widen_into(own_wide_ref, own_ref)
    widen_into(near_wide_ref, near_ref)
    blocks = ((own_ref, own_wide_ref), (near_ref, near_wide_ref))
    biases = [bias_row(ref) for ref, _ in blocks]
    for step in range(TILES):
        q = query_tile(q_ref, step)
        found = [one_block(q, *block, bias) for block, bias in zip(blocks, biases)]
        peak = jnp.maximum(found[0][2], found[1][2])
        out, total = combine(found, peak)
        out_ref[0, step] = out
        out_ref[1, step] = total
        out_ref[2, step] = peak


def finish_kernel(q_ref, got_ref, far_ref, so_far_ref, out_ref, got_wide_ref, far_wide_ref):
    widen_into(got_wide_ref, got_ref)
    widen_into(far_wide_ref, far_ref)
    got_bias, far_bias = bias_row(got_ref), bias_row(far_ref)
    resp = tail_rows(far_ref)[2:3]
    part = lane_ids((TILE, HS)) // PAIRS
    pair = lax.broadcasted_iota(jnp.int32, (4, PAIRS, HS), 1)
    diagonal = lane_ids((4, PAIRS, HS)) % PAIRS == pair
    sub = lax.broadcasted_iota(jnp.int32, (4, 8, HS), 1)

    def by_slot(x):
        x = x.reshape(8, 2, 8, HS)
        low, high = interleave(x[:, 0], x[:, 1])
        x = jnp.stack([low.reshape(2, 2, 2, 8, HS), high.reshape(2, 2, 2, 8, HS)], axis=1)
        return x.transpose(2, 1, 0, 3, 4, 5).reshape(4, PAIRS, HS)

    for step in range(TILES):
        q = query_tile(q_ref, step)
        found = [
            (so_far_ref[0, step], so_far_ref[1, step], so_far_ref[2, step]),
            one_block(q, got_ref, got_wide_ref, got_bias),
            one_block(q, far_ref, far_wide_ref, far_bias),
        ]
        ref = jnp.maximum(jnp.maximum(found[0][2], found[1][2]), found[2][2]).astype(jnp.bfloat16).astype(jnp.float32)
        out, total = combine(found, ref)
        high = total.astype(jnp.bfloat16).astype(jnp.float32)
        stats = jnp.where(part == 1, high, jnp.where(part == 2, total - high, resp))
        stats = jnp.where(part == 0, ref, stats)
        stats = jnp.where(diagonal, by_slot(stats), 0.0)
        stats = jnp.sum(stats, axis=1, keepdims=True)
        stats = jnp.where(sub == 0, stats, 0.0)
        full = jnp.concatenate([by_slot(out), stats], axis=1).reshape(4 * SLOT_ROWS, HS)
        place = (2 * step + FIRST_Y - LAST_Z) % NZ * 2 * SLOT_ROWS
        out_ref[place : place + 4 * SLOT_ROWS, :] = full.astype(jnp.bfloat16)


def merge_kernel(parts_ref, out_ref):
    parts = parts_ref[...].astype(jnp.float32).reshape(SRC, SLOT_ROWS, HS)
    resp = parts[0, PAIRS : PAIRS + 1, 3 * PAIRS : 3 * PAIRS + 1].astype(jnp.int32)
    stats = parts[:, PAIRS, :]
    stats = jnp.concatenate([stats, jnp.zeros((HS - SRC, HS), jnp.float32)], axis=0).T
    valid = lane_ids((PAIRS, HS)) < SRC
    peaks = jnp.where(valid, stats[:PAIRS], -jnp.inf)
    sums = stats[PAIRS : 2 * PAIRS] + stats[2 * PAIRS : 3 * PAIRS]
    peak = jnp.max(peaks, axis=1, keepdims=True)
    scale = jnp.exp2((peaks - peak) * EXP2_SCALE)
    denom = jnp.sum(scale * sums, axis=1, keepdims=True)
    numer = parts[0, :PAIRS] * scale[:, 0:1]
    for src in range(1, SRC):
        numer = numer + parts[src, :PAIRS] * scale[:, src : src + 1]
    result = numer / denom
    rows = PAIRS // 8
    row = lax.broadcasted_iota(jnp.int32, (rows, HS), 0)
    live = row + rows * lax.axis_index(("z", "x", "core")) < resp
    for place in range(8):
        block = result[rows * place : rows * (place + 1)]
        head = NC * HEAD_X[place // NC] + place % NC
        out_ref[:, HS * head : HS * (head + 1)] = jnp.where(live, block, 0.0).astype(jnp.bfloat16)


VMEM = pl.BlockSpec(memory_space=pltpu.VMEM)
SMEM = pl.BlockSpec(memory_space=pltpu.SMEM)
HBM = pl.BlockSpec(memory_space=pltpu.HBM)


def query_slots(queries):
    return pl.pallas_call(
        slots_kernel,
        out_shape=jax.ShapeDtypeStruct((NZ, PAIRS, HS), jnp.bfloat16),
        in_specs=[VMEM],
        out_specs=VMEM,
        compiler_params=pltpu.CompilerParams(vmem_limit_bytes=2**20),
    )(queries)


def pack(counts, resp_len, keys, values, after):
    return pl.pallas_call(
        pack_kernel,
        out_shape=jax.ShapeDtypeStruct((SEND_ROWS, HS), jnp.bfloat16),
        in_specs=[SMEM, SMEM, HBM, HBM, HBM],
        out_specs=VMEM,
        scratch_shapes=[pltpu.SemaphoreType.DMA((2,))],
        compiler_params=pltpu.CompilerParams(vmem_limit_bytes=2 * 2**20),
        cost_estimate=pl.CostEstimate(flops=0, bytes_accessed=2**23, transcendentals=0),
    )(counts, resp_len, keys, values, after)


def turn(groups):
    return pl.pallas_call(
        turn_kernel,
        out_shape=jax.ShapeDtypeStruct((2, NY, PAIRS, HS), jnp.bfloat16),
        in_specs=[VMEM],
        out_specs=VMEM,
        compiler_params=pltpu.CompilerParams(vmem_limit_bytes=2**20),
        cost_estimate=pl.CostEstimate(flops=2**36, bytes_accessed=2**21, transcendentals=0),
    )(groups)


def attend(spread, own, near):
    return pl.pallas_call(
        attend_kernel,
        out_shape=jax.ShapeDtypeStruct((3, TILES, TILE, HS), jnp.float32),
        in_specs=[VMEM] * 3,
        out_specs=VMEM,
        scratch_shapes=[pltpu.VMEM((SLOTS, 2 * HS), jnp.bfloat16)] * 2,
        compiler_params=pltpu.CompilerParams(vmem_limit_bytes=12 * 2**20),
        cost_estimate=pl.CostEstimate(flops=2**34, bytes_accessed=2**21, transcendentals=0),
    )(spread, own, near)


def finish(spread, got, far, so_far):
    return pl.pallas_call(
        finish_kernel,
        out_shape=jax.ShapeDtypeStruct((SRC * SLOT_ROWS, HS), jnp.bfloat16),
        in_specs=[VMEM] * 4,
        out_specs=VMEM,
        scratch_shapes=[pltpu.VMEM((SLOTS, 2 * HS), jnp.bfloat16)] * 2,
        compiler_params=pltpu.CompilerParams(vmem_limit_bytes=8 * 2**20),
    )(spread, got, far, so_far)


def merge(parts):
    return pl.pallas_call(
        merge_kernel,
        out_shape=jax.ShapeDtypeStruct((4, 8 * HS), jnp.bfloat16),
        in_specs=[VMEM],
        out_specs=VMEM,
        compiler_params=pltpu.CompilerParams(vmem_limit_bytes=4 * 2**20),
    )(parts)


def local(queries, keys, values, counts, resp_len):
    swap_cores = [(0, 1), (1, 0)]
    swap_chips = [way for a, b in SHARERS for way in ((a, b), (b, a))]
    with jax.named_scope("query_spread"):
        slots = query_slots(queries)
        groups = exchange(slots.reshape(NZ * 4, 8, HS), groups_spread()).reshape(NZ, PAIRS, HS)
    with jax.named_scope("block_exchange"):
        own = pack(counts, resp_len, keys, values, slots)
        near = lax.ppermute(own, "x", swap_chips)
        got = lax.ppermute(own, "core", swap_cores)
        far = lax.ppermute(near, "core", swap_cores)
    groups, own = lax.optimization_barrier((groups, own))
    with jax.named_scope("query_turn"):
        groups = turn(groups).reshape(SRC, PAIRS, HS)
        spread = exchange(groups, groups_turn()).reshape(2, NY, PAIRS, HS)
    with jax.named_scope("attend"):
        so_far = attend(spread, own, near)
        parts = finish(spread, got, far, so_far)
    with jax.named_scope("merge"):
        parts = exchange(parts.reshape(SRC, SLOT_ROWS, HS), groups_merge())
        return merge(parts.reshape(SRC * SLOT_ROWS, HS))


def solution(mesh):
    grid = Mesh(mesh.devices.reshape(NZ, NX, NC, NY), ("z", "x", "core", "tp"))
    ctx = ("z", "x", "core")
    in_specs = (P("tp", ctx), P(ctx, "tp"), P(ctx, "tp"), P(ctx), P())
    return jax.shard_map(
        local, mesh=grid, in_specs=in_specs, out_specs=P(ctx, "tp"), check_vma=False
    )
```

```python
import jax
import jax.numpy as jnp
from jax import lax
from jax.experimental import pallas as pl
from jax.experimental.pallas import tpu as pltpu
from jax.sharding import Mesh, PartitionSpec as P

HS = 128
LOG2E = 1.4426950408889634
EXP2_SCALE = LOG2E / HS**0.5
NZ, NX, NC, NY = 8, 4, 2, 8
SLOTS = 1024
TILE = 128
TILES = 4
PAIRS = 32
SLOT_ROWS = 40
SRC = NZ * 2
SEND_ROWS = 2 * SLOTS + 16
COUNT_BASE = 64
MASKED = -1e30
FIRST_Z, FIRST_Y, LAST_Z = 6, 4, 4
SHARERS = ((0, 1), (3, 2))
CLASSES = ((3, 0), (2, 1))
HEAD_X = (3, 2, 0, 1)


def lane_ids(shape):
    return lax.broadcasted_iota(jnp.int32, shape, len(shape) - 1)


def device(z, x, core, y):
    return ((z % NZ * NX + x % NX) * NC + core) * NY + y % NY


def groups_spread():
    return [
        [device(z + FIRST_Z, x, core, y) for z in range(NZ) for x in pair for core in range(NC)]
        for pair in SHARERS
        for y in range(NY)
    ]


def groups_turn():
    return [
        [device(z, x, core, y + FIRST_Y) for x in pair for y in range(NY)]
        for z in range(NZ)
        for core in range(NC)
        for pair in CLASSES
    ]


def groups_merge():
    return [
        [device(z + LAST_Z, x, core, y) for z in range(NZ) for x in pair]
        for core in range(NC)
        for y in range(NY)
        for pair in CLASSES
    ]


def exchange(blocks, groups):
    axes = ("z", "x", "core", "tp")
    return lax.all_to_all(blocks, axes, 0, 0, axis_index_groups=groups, tiled=True)


def interleave(first, second):
    low = jnp.concatenate([first[:, :4], second[:, :4]], axis=1)
    high = jnp.concatenate([first[:, 4:], second[:, 4:]], axis=1)
    return low, high


def pack_kernel(query_ref, key_ref, value_ref, slots_ref, send_ref, rows, slots, both, sems):
    def copy(source, target, which):
        made = pltpu.make_async_copy(source, target, sems.at[which])
        made.start()
        return made

    first, second = pl.ds(0, SLOTS), pl.ds(SLOTS, SLOTS)
    loads = (
        copy(query_ref, rows, 0),
        copy(key_ref, both.at[first], 1),
        copy(value_ref, both.at[second], 2),
    )
    loads[0].wait()
    by_x = rows[...].astype(jnp.float32).reshape(NX, 8, HS)
    parts = []
    for upper, lower in CLASSES:
        parts += interleave(by_x[upper : upper + 1], by_x[lower : lower + 1])
    block = jnp.concatenate(parts, axis=0).reshape(PAIRS, HS).astype(jnp.bfloat16)
    for z in range(NZ):
        slots[z] = block
    stores = [copy(slots, slots_ref, 3)]
    for which, part in enumerate((first, second)):
        loads[1 + which].wait()
        stores.append(copy(both.at[part], send_ref.at[part], 4 + which))
    for store in stores:
        store.wait()


def note_kernel(count_ref, resp_ref, _, send_ref, tail_ref, sem):
    count = count_ref[0]
    row = lax.broadcasted_iota(jnp.int32, (16, HS), 0)
    high = count // COUNT_BASE
    tail = jnp.where(row == 0, high, jnp.where(row == 1, count - high * COUNT_BASE, resp_ref[0]))
    tail_ref[...] = tail.astype(jnp.float32).astype(jnp.bfloat16)
    copy = pltpu.make_async_copy(tail_ref, send_ref.at[pl.ds(2 * SLOTS, 16)], sem)
    copy.start()
    copy.wait()


def turn_kernel(groups_ref, turned_ref):
    for place in range(NY):
        block = groups_ref[(place + FIRST_Y - FIRST_Z) % NZ]
        for x in range(2):
            turned_ref[x, place] = block


def widen_into(wide_ref, ref):
    wide_ref[:, :HS] = ref[SLOTS : 2 * SLOTS, :]
    wide_ref[:, HS:] = jnp.ones((SLOTS, HS), jnp.bfloat16)


def tail_rows(ref):
    return ref[2 * SLOTS : SEND_ROWS, :].astype(jnp.float32)


def bias_row(ref):
    tail = tail_rows(ref)
    count = tail[0:1] * COUNT_BASE + tail[1:2]
    count = jnp.concatenate([count] * (SLOTS // HS), axis=1).astype(jnp.int32)
    return jnp.where(lane_ids((1, SLOTS)) < count, 0.0, MASKED)


def one_block(q, ref, wide_ref, bias):
    scores = lax.dot_general(
        q, ref[:SLOTS, :], (((1,), (1,)), ((), ())), preferred_element_type=jnp.float32
    )
    scores = scores + bias
    peak = jnp.max(scores, axis=1, keepdims=True)
    weights = jnp.exp2((scores - peak) * EXP2_SCALE).astype(jnp.bfloat16)
    both = jnp.dot(weights, wide_ref[...], preferred_element_type=jnp.float32)
    return both[:, :HS], both[:, HS:], jnp.broadcast_to(peak, (TILE, HS))


def combine(found, ref):
    out, total = 0.0, 0.0
    for block_out, block_sum, peak in found:
        scale = jnp.exp2((peak - ref) * EXP2_SCALE)
        out = out + block_out * scale
        total = total + block_sum * scale
    return out, total


def query_tile(q_ref, step):
    return q_ref[:, 2 * step : 2 * step + 2].reshape(TILE, HS)


def attend_kernel(q_ref, own_ref, near_ref, out_ref, own_wide_ref, near_wide_ref):
    widen_into(own_wide_ref, own_ref)
    widen_into(near_wide_ref, near_ref)
    blocks = ((own_ref, own_wide_ref), (near_ref, near_wide_ref))
    biases = [bias_row(ref) for ref, _ in blocks]
    for step in range(TILES):
        q = query_tile(q_ref, step)
        found = [one_block(q, *block, bias) for block, bias in zip(blocks, biases)]
        peak = jnp.maximum(found[0][2], found[1][2])
        out, total = combine(found, peak)
        out_ref[0, step] = out
        out_ref[1, step] = total
        out_ref[2, step] = peak


def finish_kernel(q_ref, got_ref, far_ref, so_far_ref, out_ref, got_wide_ref, far_wide_ref):
    widen_into(got_wide_ref, got_ref)
    widen_into(far_wide_ref, far_ref)
    got_bias, far_bias = bias_row(got_ref), bias_row(far_ref)
    resp = tail_rows(far_ref)[2:3]
    part = lane_ids((TILE, HS)) // PAIRS
    pair = lax.broadcasted_iota(jnp.int32, (4, PAIRS, HS), 1)
    diagonal = lane_ids((4, PAIRS, HS)) % PAIRS == pair
    sub = lax.broadcasted_iota(jnp.int32, (4, 8, HS), 1)

    def by_slot(x):
        x = x.reshape(8, 2, 8, HS)
        low, high = interleave(x[:, 0], x[:, 1])
        x = jnp.stack([low.reshape(2, 2, 2, 8, HS), high.reshape(2, 2, 2, 8, HS)], axis=1)
        return x.transpose(2, 1, 0, 3, 4, 5).reshape(4, PAIRS, HS)

    for step in range(TILES):
        q = query_tile(q_ref, step)
        found = [
            (so_far_ref[0, step], so_far_ref[1, step], so_far_ref[2, step]),
            one_block(q, got_ref, got_wide_ref, got_bias),
            one_block(q, far_ref, far_wide_ref, far_bias),
        ]
        ref = jnp.maximum(jnp.maximum(found[0][2], found[1][2]), found[2][2]).astype(jnp.bfloat16).astype(jnp.float32)
        out, total = combine(found, ref)
        high = total.astype(jnp.bfloat16).astype(jnp.float32)
        stats = jnp.where(part == 1, high, jnp.where(part == 2, total - high, resp))
        stats = jnp.where(part == 0, ref, stats)
        stats = jnp.where(diagonal, by_slot(stats), 0.0)
        stats = jnp.sum(stats, axis=1, keepdims=True)
        stats = jnp.where(sub == 0, stats, 0.0)
        full = jnp.concatenate([by_slot(out), stats], axis=1).reshape(4 * SLOT_ROWS, HS)
        place = (2 * step + FIRST_Y - LAST_Z) % NZ * 2 * SLOT_ROWS
        out_ref[place : place + 4 * SLOT_ROWS, :] = full.astype(jnp.bfloat16)


def merge_kernel(parts_ref, out_ref):
    parts = parts_ref[...].astype(jnp.float32).reshape(SRC, SLOT_ROWS, HS)
    resp = parts[0, PAIRS : PAIRS + 1, 3 * PAIRS : 3 * PAIRS + 1].astype(jnp.int32)
    stats = parts[:, PAIRS, :]
    stats = jnp.concatenate([stats, jnp.zeros((HS - SRC, HS), jnp.float32)], axis=0).T
    valid = lane_ids((PAIRS, HS)) < SRC
    peaks = jnp.where(valid, stats[:PAIRS], -jnp.inf)
    sums = stats[PAIRS : 2 * PAIRS] + stats[2 * PAIRS : 3 * PAIRS]
    peak = jnp.max(peaks, axis=1, keepdims=True)
    scale = jnp.exp2((peaks - peak) * EXP2_SCALE)
    denom = jnp.sum(scale * sums, axis=1, keepdims=True)
    numer = parts[0, :PAIRS] * scale[:, 0:1]
    for src in range(1, SRC):
        numer = numer + parts[src, :PAIRS] * scale[:, src : src + 1]
    result = numer / denom
    rows = PAIRS // 8
    row = lax.broadcasted_iota(jnp.int32, (rows, HS), 0)
    live = row + rows * lax.axis_index(("z", "x", "core")) < resp
    for place in range(8):
        block = result[rows * place : rows * (place + 1)]
        head = NC * HEAD_X[place // NC] + place % NC
        out_ref[:, HS * head : HS * (head + 1)] = jnp.where(live, block, 0.0).astype(jnp.bfloat16)


VMEM = pl.BlockSpec(memory_space=pltpu.VMEM)
SMEM = pl.BlockSpec(memory_space=pltpu.SMEM)
HBM = pl.BlockSpec(memory_space=pltpu.HBM)


def pack(queries, keys, values):
    return pl.pallas_call(
        pack_kernel,
        out_shape=(
            jax.ShapeDtypeStruct((NZ, PAIRS, HS), jnp.bfloat16),
            jax.ShapeDtypeStruct((SEND_ROWS, HS), jnp.bfloat16),
        ),
        in_specs=[HBM] * 3,
        out_specs=(HBM, HBM),
        scratch_shapes=[
            pltpu.VMEM((PAIRS, HS), jnp.bfloat16),
            pltpu.VMEM((NZ, PAIRS, HS), jnp.bfloat16),
            pltpu.VMEM((2 * SLOTS, HS), jnp.bfloat16),
            pltpu.SemaphoreType.DMA((6,)),
        ],
        compiler_params=pltpu.CompilerParams(vmem_limit_bytes=60 * 2**20),
    )(queries, keys, values)


def note(counts, resp_len, own):
    return pl.pallas_call(
        note_kernel,
        out_shape=jax.ShapeDtypeStruct((SEND_ROWS, HS), jnp.bfloat16),
        in_specs=[SMEM, SMEM, HBM],
        out_specs=HBM,
        input_output_aliases={2: 0},
        scratch_shapes=[pltpu.VMEM((16, HS), jnp.bfloat16), pltpu.SemaphoreType.DMA],
        compiler_params=pltpu.CompilerParams(vmem_limit_bytes=60 * 2**20),
    )(counts, resp_len, own)


def turn(groups):
    return pl.pallas_call(
        turn_kernel,
        out_shape=jax.ShapeDtypeStruct((2, NY, PAIRS, HS), jnp.bfloat16),
        in_specs=[VMEM],
        out_specs=VMEM,
        compiler_params=pltpu.CompilerParams(vmem_limit_bytes=2**20),
        cost_estimate=pl.CostEstimate(flops=2**36, bytes_accessed=2**21, transcendentals=0),
    )(groups)


def attend(spread, own, near):
    return pl.pallas_call(
        attend_kernel,
        out_shape=jax.ShapeDtypeStruct((3, TILES, TILE, HS), jnp.float32),
        in_specs=[VMEM] * 3,
        out_specs=VMEM,
        scratch_shapes=[pltpu.VMEM((SLOTS, 2 * HS), jnp.bfloat16)] * 2,
        compiler_params=pltpu.CompilerParams(vmem_limit_bytes=12 * 2**20),
        cost_estimate=pl.CostEstimate(flops=2**34, bytes_accessed=2**21, transcendentals=0),
    )(spread, own, near)


def finish(spread, got, far, so_far):
    return pl.pallas_call(
        finish_kernel,
        out_shape=jax.ShapeDtypeStruct((SRC * SLOT_ROWS, HS), jnp.bfloat16),
        in_specs=[VMEM] * 4,
        out_specs=VMEM,
        scratch_shapes=[pltpu.VMEM((SLOTS, 2 * HS), jnp.bfloat16)] * 2,
        compiler_params=pltpu.CompilerParams(vmem_limit_bytes=8 * 2**20),
    )(spread, got, far, so_far)


def merge(parts):
    return pl.pallas_call(
        merge_kernel,
        out_shape=jax.ShapeDtypeStruct((4, 8 * HS), jnp.bfloat16),
        in_specs=[VMEM],
        out_specs=VMEM,
        compiler_params=pltpu.CompilerParams(vmem_limit_bytes=4 * 2**20),
    )(parts)


def local(queries, keys, values, counts, resp_len):
    swap_cores = [(0, 1), (1, 0)]
    swap_chips = [way for a, b in SHARERS for way in ((a, b), (b, a))]
    with jax.named_scope("query_spread"):
        slots, own = pack(queries, keys, values)
        groups = exchange(slots.reshape(NZ * 4, 8, HS), groups_spread()).reshape(NZ, PAIRS, HS)
    with jax.named_scope("block_exchange"):
        own = note(counts, resp_len, own)
        near = lax.ppermute(own, "x", swap_chips)
        got = lax.ppermute(own, "core", swap_cores)
        far = lax.ppermute(near, "core", swap_cores)
    groups, own = lax.optimization_barrier((groups, own))
    with jax.named_scope("query_turn"):
        groups = turn(groups).reshape(SRC, PAIRS, HS)
        spread = exchange(groups, groups_turn()).reshape(2, NY, PAIRS, HS)
    with jax.named_scope("attend"):
        so_far = attend(spread, own, near)
        parts = finish(spread, got, far, so_far)
    with jax.named_scope("merge"):
        parts = exchange(parts.reshape(SRC, SLOT_ROWS, HS), groups_merge())
        return merge(parts.reshape(SRC * SLOT_ROWS, HS))


def solution(mesh):
    grid = Mesh(mesh.devices.reshape(NZ, NX, NC, NY), ("z", "x", "core", "tp"))
    ctx = ("z", "x", "core")
    in_specs = (P("tp", ctx), P(ctx, "tp"), P(ctx, "tp"), P(ctx), P())
    return jax.shard_map(
        local, mesh=grid, in_specs=in_specs, out_specs=P(ctx, "tp"), check_vma=False
    )
```

```python
import jax
import jax.numpy as jnp
from jax import lax
from jax.experimental import pallas as pl
from jax.experimental.pallas import tpu as pltpu
from jax.sharding import Mesh, PartitionSpec as P

HS = 128
LOG2E = 1.4426950408889634
EXP2_SCALE = LOG2E / HS**0.5
NZ, NX, NC, NY = 8, 4, 2, 8
SLOTS = 1024
TILE = 128
TILES = 4
PAIRS = 32
SLOT_ROWS = 40
SRC = NZ * 2
SEND_ROWS = 2 * SLOTS + 16
COUNT_BASE = 64
MASKED = -1e30
FIRST_Z, FIRST_Y, LAST_Z = 5, 5, 5
SHARERS = ((0, 1), (3, 2))
CLASSES = ((3, 0), (2, 1))
HEAD_X = (3, 2, 0, 1)


def lane_ids(shape):
    return lax.broadcasted_iota(jnp.int32, shape, len(shape) - 1)


def device(z, x, core, y):
    return ((z % NZ * NX + x % NX) * NC + core) * NY + y % NY


def groups_spread():
    return [
        [device(z + FIRST_Z, x, core, y) for z in range(NZ) for x in pair for core in range(NC)]
        for pair in SHARERS
        for y in range(NY)
    ]


def groups_turn():
    return [
        [device(z, x, core, y + FIRST_Y) for x in pair for y in range(NY)]
        for z in range(NZ)
        for core in range(NC)
        for pair in CLASSES
    ]


def groups_merge():
    return [
        [device(z + LAST_Z, x, core, y) for z in range(NZ) for x in pair]
        for core in range(NC)
        for y in range(NY)
        for pair in CLASSES
    ]


def exchange(blocks, groups):
    axes = ("z", "x", "core", "tp")
    return lax.all_to_all(blocks, axes, 0, 0, axis_index_groups=groups, tiled=True)


def interleave(first, second):
    low = jnp.concatenate([first[:, :4], second[:, :4]], axis=1)
    high = jnp.concatenate([first[:, 4:], second[:, 4:]], axis=1)
    return low, high


def pack_kernel(
    count_ref, query_ref, key_ref, value_ref, slots_ref, send_ref, rows, slots, both, tail, sems
):
    def copy(source, target, which):
        made = pltpu.make_async_copy(source, target, sems.at[which])
        made.start()
        return made

    first, second = pl.ds(0, SLOTS), pl.ds(SLOTS, SLOTS)
    loads = (
        copy(query_ref, rows, 0),
        copy(key_ref, both.at[first], 1),
        copy(value_ref, both.at[second], 2),
    )
    loads[0].wait()
    by_x = rows[...].astype(jnp.float32).reshape(NX, 8, HS)
    parts = []
    for upper, lower in CLASSES:
        parts += interleave(by_x[upper : upper + 1], by_x[lower : lower + 1])
    block = jnp.concatenate(parts, axis=0).reshape(PAIRS, HS).astype(jnp.bfloat16)
    for z in range(NZ):
        slots[z] = block
    count = count_ref[0]
    row = lax.broadcasted_iota(jnp.int32, (16, HS), 0)
    high = count // COUNT_BASE
    tail[...] = jnp.where(row == 0, high, count - high * COUNT_BASE).astype(jnp.float32).astype(jnp.bfloat16)
    stores = [copy(slots, slots_ref, 3), copy(tail, send_ref.at[pl.ds(2 * SLOTS, 16)], 6)]
    for which, part in enumerate((first, second)):
        loads[1 + which].wait()
        stores.append(copy(both.at[part], send_ref.at[part], 4 + which))
    for store in stores:
        store.wait()


def turn_kernel(resp_ref, groups_ref, turned_ref, noted_ref):
    noted_ref[...] = jnp.full((8, HS), resp_ref[0], jnp.int32).astype(jnp.float32)
    for place in range(NY):
        block = groups_ref[(place + FIRST_Y - FIRST_Z) % NZ]
        for x in range(2):
            turned_ref[x, place] = block


def widen_into(wide_ref, ref):
    wide_ref[:, :HS] = ref[SLOTS : 2 * SLOTS, :]
    wide_ref[:, HS:] = jnp.ones((SLOTS, HS), jnp.bfloat16)


def tail_rows(ref):
    return ref[2 * SLOTS : SEND_ROWS, :].astype(jnp.float32)


def bias_row(ref):
    tail = tail_rows(ref)
    count = tail[0:1] * COUNT_BASE + tail[1:2]
    count = jnp.concatenate([count] * (SLOTS // HS), axis=1).astype(jnp.int32)
    return jnp.where(lane_ids((1, SLOTS)) < count, 0.0, MASKED)


def one_block(q, ref, wide_ref, bias):
    scores = lax.dot_general(
        q, ref[:SLOTS, :], (((1,), (1,)), ((), ())), preferred_element_type=jnp.float32
    )
    scores = scores + bias
    peak = jnp.max(scores, axis=1, keepdims=True)
    weights = jnp.exp2((scores - peak) * EXP2_SCALE).astype(jnp.bfloat16)
    both = jnp.dot(weights, wide_ref[...], preferred_element_type=jnp.float32)
    return both[:, :HS], both[:, HS:], jnp.broadcast_to(peak, (TILE, HS))


def combine(found, ref):
    out, total = 0.0, 0.0
    for block_out, block_sum, peak in found:
        scale = jnp.exp2((peak - ref) * EXP2_SCALE)
        out = out + block_out * scale
        total = total + block_sum * scale
    return out, total


def query_tile(q_ref, step):
    return q_ref[:, 2 * step : 2 * step + 2].reshape(TILE, HS)


def attend_kernel(q_ref, own_ref, near_ref, out_ref, own_wide_ref, near_wide_ref):
    widen_into(own_wide_ref, own_ref)
    widen_into(near_wide_ref, near_ref)
    blocks = ((own_ref, own_wide_ref), (near_ref, near_wide_ref))
    biases = [bias_row(ref) for ref, _ in blocks]
    for step in range(TILES):
        q = query_tile(q_ref, step)
        found = [one_block(q, *block, bias) for block, bias in zip(blocks, biases)]
        peak = jnp.maximum(found[0][2], found[1][2])
        out, total = combine(found, peak)
        out_ref[0, step] = out
        out_ref[1, step] = total
        out_ref[2, step] = peak


def finish_kernel(
    q_ref, got_ref, far_ref, so_far_ref, resp_ref, out_ref, got_wide_ref, far_wide_ref
):
    widen_into(got_wide_ref, got_ref)
    widen_into(far_wide_ref, far_ref)
    got_bias, far_bias = bias_row(got_ref), bias_row(far_ref)
    resp = resp_ref[0:1]
    part = lane_ids((TILE, HS)) // PAIRS
    pair = lax.broadcasted_iota(jnp.int32, (4, PAIRS, HS), 1)
    diagonal = lane_ids((4, PAIRS, HS)) % PAIRS == pair
    sub = lax.broadcasted_iota(jnp.int32, (4, 8, HS), 1)

    def by_slot(x):
        x = x.reshape(8, 2, 8, HS)
        low, high = interleave(x[:, 0], x[:, 1])
        x = jnp.stack([low.reshape(2, 2, 2, 8, HS), high.reshape(2, 2, 2, 8, HS)], axis=1)
        return x.transpose(2, 1, 0, 3, 4, 5).reshape(4, PAIRS, HS)

    for step in range(TILES):
        q = query_tile(q_ref, step)
        found = [
            (so_far_ref[0, step], so_far_ref[1, step], so_far_ref[2, step]),
            one_block(q, got_ref, got_wide_ref, got_bias),
            one_block(q, far_ref, far_wide_ref, far_bias),
        ]
        ref = jnp.maximum(jnp.maximum(found[0][2], found[1][2]), found[2][2]).astype(jnp.bfloat16).astype(jnp.float32)
        out, total = combine(found, ref)
        high = total.astype(jnp.bfloat16).astype(jnp.float32)
        stats = jnp.where(part == 1, high, jnp.where(part == 2, total - high, resp))
        stats = jnp.where(part == 0, ref, stats)
        stats = jnp.where(diagonal, by_slot(stats), 0.0)
        stats = jnp.sum(stats, axis=1, keepdims=True)
        stats = jnp.where(sub == 0, stats, 0.0)
        full = jnp.concatenate([by_slot(out), stats], axis=1).reshape(4 * SLOT_ROWS, HS)
        place = (2 * step + FIRST_Y - LAST_Z) % NZ * 2 * SLOT_ROWS
        out_ref[place : place + 4 * SLOT_ROWS, :] = full.astype(jnp.bfloat16)


def merge_kernel(parts_ref, out_ref):
    parts = parts_ref[...].astype(jnp.float32).reshape(SRC, SLOT_ROWS, HS)
    resp = parts[0, PAIRS : PAIRS + 1, 3 * PAIRS : 3 * PAIRS + 1].astype(jnp.int32)
    stats = parts[:, PAIRS, :]
    stats = jnp.concatenate([stats, jnp.zeros((HS - SRC, HS), jnp.float32)], axis=0).T
    valid = lane_ids((PAIRS, HS)) < SRC
    peaks = jnp.where(valid, stats[:PAIRS], -jnp.inf)
    sums = stats[PAIRS : 2 * PAIRS] + stats[2 * PAIRS : 3 * PAIRS]
    peak = jnp.max(peaks, axis=1, keepdims=True)
    scale = jnp.exp2((peaks - peak) * EXP2_SCALE)
    denom = jnp.sum(scale * sums, axis=1, keepdims=True)
    numer = parts[0, :PAIRS] * scale[:, 0:1]
    for src in range(1, SRC):
        numer = numer + parts[src, :PAIRS] * scale[:, src : src + 1]
    result = numer / denom
    rows = PAIRS // 8
    row = lax.broadcasted_iota(jnp.int32, (rows, HS), 0)
    live = row + rows * lax.axis_index(("z", "x", "core")) < resp
    for place in range(8):
        block = result[rows * place : rows * (place + 1)]
        head = NC * HEAD_X[place // NC] + place % NC
        out_ref[:, HS * head : HS * (head + 1)] = jnp.where(live, block, 0.0).astype(jnp.bfloat16)


VMEM = pl.BlockSpec(memory_space=pltpu.VMEM)
SMEM = pl.BlockSpec(memory_space=pltpu.SMEM)
HBM = pl.BlockSpec(memory_space=pltpu.HBM)


def pack(counts, queries, keys, values):
    return pl.pallas_call(
        pack_kernel,
        out_shape=(
            jax.ShapeDtypeStruct((NZ, PAIRS, HS), jnp.bfloat16),
            jax.ShapeDtypeStruct((SEND_ROWS, HS), jnp.bfloat16),
        ),
        in_specs=[SMEM, HBM, HBM, HBM],
        out_specs=(HBM, HBM),
        scratch_shapes=[
            pltpu.VMEM((PAIRS, HS), jnp.bfloat16),
            pltpu.VMEM((NZ, PAIRS, HS), jnp.bfloat16),
            pltpu.VMEM((2 * SLOTS, HS), jnp.bfloat16),
            pltpu.VMEM((16, HS), jnp.bfloat16),
            pltpu.SemaphoreType.DMA((7,)),
        ],
        compiler_params=pltpu.CompilerParams(vmem_limit_bytes=60 * 2**20),
    )(counts, queries, keys, values)


def turn(resp_len, groups):
    return pl.pallas_call(
        turn_kernel,
        out_shape=(
            jax.ShapeDtypeStruct((2, NY, PAIRS, HS), jnp.bfloat16),
            jax.ShapeDtypeStruct((8, HS), jnp.float32),
        ),
        in_specs=[SMEM, VMEM],
        out_specs=(VMEM, VMEM),
        compiler_params=pltpu.CompilerParams(vmem_limit_bytes=2**20),
        cost_estimate=pl.CostEstimate(flops=2**36, bytes_accessed=2**21, transcendentals=0),
    )(resp_len, groups)


def attend(spread, own, near):
    return pl.pallas_call(
        attend_kernel,
        out_shape=jax.ShapeDtypeStruct((3, TILES, TILE, HS), jnp.float32),
        in_specs=[VMEM] * 3,
        out_specs=VMEM,
        scratch_shapes=[pltpu.VMEM((SLOTS, 2 * HS), jnp.bfloat16)] * 2,
        compiler_params=pltpu.CompilerParams(vmem_limit_bytes=12 * 2**20),
        cost_estimate=pl.CostEstimate(flops=2**34, bytes_accessed=2**21, transcendentals=0),
    )(spread, own, near)


def finish(spread, got, far, so_far, resp):
    return pl.pallas_call(
        finish_kernel,
        out_shape=jax.ShapeDtypeStruct((SRC * SLOT_ROWS, HS), jnp.bfloat16),
        in_specs=[VMEM] * 5,
        out_specs=VMEM,
        scratch_shapes=[pltpu.VMEM((SLOTS, 2 * HS), jnp.bfloat16)] * 2,
        compiler_params=pltpu.CompilerParams(vmem_limit_bytes=8 * 2**20),
    )(spread, got, far, so_far, resp)


def merge(parts):
    return pl.pallas_call(
        merge_kernel,
        out_shape=jax.ShapeDtypeStruct((4, 8 * HS), jnp.bfloat16),
        in_specs=[VMEM],
        out_specs=VMEM,
        compiler_params=pltpu.CompilerParams(vmem_limit_bytes=4 * 2**20),
    )(parts)


def local(queries, keys, values, counts, resp_len):
    swap_cores = [(0, 1), (1, 0)]
    swap_chips = [way for a, b in SHARERS for way in ((a, b), (b, a))]
    with jax.named_scope("query_spread"):
        slots, own = pack(counts, queries, keys, values)
        groups = exchange(slots.reshape(NZ * 4, 8, HS), groups_spread()).reshape(NZ, PAIRS, HS)
    with jax.named_scope("block_exchange"):
        near = lax.ppermute(own, "x", swap_chips)
        got = lax.ppermute(own, "core", swap_cores)
        far = lax.ppermute(near, "core", swap_cores)
    groups, own = lax.optimization_barrier((groups, own))
    with jax.named_scope("query_turn"):
        turned, resp = turn(resp_len, groups)
        spread = exchange(turned.reshape(SRC, PAIRS, HS), groups_turn()).reshape(2, NY, PAIRS, HS)
    with jax.named_scope("attend"):
        so_far = attend(spread, own, near)
        parts = finish(spread, got, far, so_far, resp)
    with jax.named_scope("merge"):
        parts = exchange(parts.reshape(SRC, SLOT_ROWS, HS), groups_merge())
        return merge(parts.reshape(SRC * SLOT_ROWS, HS))


def solution(mesh):
    grid = Mesh(mesh.devices.reshape(NZ, NX, NC, NY), ("z", "x", "core", "tp"))
    ctx = ("z", "x", "core")
    in_specs = (P("tp", ctx), P(ctx, "tp"), P(ctx, "tp"), P(ctx), P())
    return jax.shard_map(
        local, mesh=grid, in_specs=in_specs, out_specs=P(ctx, "tp"), check_vma=False
    )
```

```python
import jax
import jax.numpy as jnp
from jax import lax
from jax.experimental import pallas as pl
from jax.experimental.pallas import tpu as pltpu
from jax.sharding import Mesh, PartitionSpec as P

HS = 128
LOG2E = 1.4426950408889634
EXP2_SCALE = LOG2E / HS**0.5
NZ, NX, NC, NY = 8, 4, 2, 8
SLOTS = 1024
TILE = 128
TILES = 4
PAIRS = 32
SLOT_ROWS = 40
SRC = NZ * 2
SEND_ROWS = 2 * SLOTS + 16
COUNT_BASE = 64
MASKED = -1e30
FIRST_Z, FIRST_Y, LAST_Z = 5, 6, 4
SHARERS = ((0, 1), (3, 2))
CLASSES = ((3, 0), (2, 1))
HEAD_X = (3, 2, 0, 1)


def lane_ids(shape):
    return lax.broadcasted_iota(jnp.int32, shape, len(shape) - 1)


def device(z, x, core, y):
    return ((z % NZ * NX + x % NX) * NC + core) * NY + y % NY


def groups_spread():
    return [
        [device(z + FIRST_Z, x, core, y) for z in range(NZ) for x in pair for core in range(NC)]
        for pair in SHARERS
        for y in range(NY)
    ]


def groups_turn():
    return [
        [device(z, x, core, y + FIRST_Y) for x in pair for y in range(NY)]
        for z in range(NZ)
        for core in range(NC)
        for pair in CLASSES
    ]


def groups_merge():
    return [
        [device(z + LAST_Z, x, core, y) for z in range(NZ) for x in pair]
        for core in range(NC)
        for y in range(NY)
        for pair in CLASSES
    ]


def exchange(blocks, groups):
    axes = ("z", "x", "core", "tp")
    return lax.all_to_all(blocks, axes, 0, 0, axis_index_groups=groups, tiled=True)


def interleave(first, second):
    low = jnp.concatenate([first[:, :4], second[:, :4]], axis=1)
    high = jnp.concatenate([first[:, 4:], second[:, 4:]], axis=1)
    return low, high


def pack_kernel(
    count_ref, query_ref, key_ref, value_ref, slots_ref, send_ref, rows, slots, both, tail, sems
):
    def copy(source, target, which):
        made = pltpu.make_async_copy(source, target, sems.at[which])
        made.start()
        return made

    first, second = pl.ds(0, SLOTS), pl.ds(SLOTS, SLOTS)
    loads = (
        copy(query_ref, rows, 0),
        copy(key_ref, both.at[first], 1),
        copy(value_ref, both.at[second], 2),
    )
    loads[0].wait()
    by_x = rows[...].astype(jnp.float32).reshape(NX, 8, HS)
    parts = []
    for upper, lower in CLASSES:
        parts += interleave(by_x[upper : upper + 1], by_x[lower : lower + 1])
    block = jnp.concatenate(parts, axis=0).reshape(PAIRS, HS).astype(jnp.bfloat16)
    for z in range(NZ):
        slots[z] = block
    count = count_ref[0]
    row = lax.broadcasted_iota(jnp.int32, (16, HS), 0)
    high = count // COUNT_BASE
    tail[...] = jnp.where(row == 0, high, count - high * COUNT_BASE).astype(jnp.float32).astype(jnp.bfloat16)
    stores = [copy(slots, slots_ref, 3), copy(tail, send_ref.at[pl.ds(2 * SLOTS, 16)], 6)]
    for which, part in enumerate((first, second)):
        loads[1 + which].wait()
        stores.append(copy(both.at[part], send_ref.at[part], 4 + which))
    for store in stores:
        store.wait()


def turn_kernel(resp_ref, groups_ref, turned_ref, noted_ref):
    noted_ref[...] = jnp.full((8, HS), resp_ref[0], jnp.int32).astype(jnp.float32)
    for place in range(NY):
        block = groups_ref[(place + FIRST_Y - FIRST_Z) % NZ]
        for x in range(2):
            turned_ref[x, place] = block


def widen_into(wide_ref, ref):
    wide_ref[:, :HS] = ref[SLOTS : 2 * SLOTS, :]
    wide_ref[:, HS:] = jnp.ones((SLOTS, HS), jnp.bfloat16)


def tail_rows(ref):
    return ref[2 * SLOTS : SEND_ROWS, :].astype(jnp.float32)


def bias_row(ref):
    tail = tail_rows(ref)
    count = tail[0:1] * COUNT_BASE + tail[1:2]
    count = jnp.concatenate([count] * (SLOTS // HS), axis=1).astype(jnp.int32)
    return jnp.where(lane_ids((1, SLOTS)) < count, 0.0, MASKED)


def one_block(q, ref, wide_ref, bias):
    scores = lax.dot_general(
        q, ref[:SLOTS, :], (((1,), (1,)), ((), ())), preferred_element_type=jnp.float32
    )
    scores = scores + bias
    peak = jnp.max(scores, axis=1, keepdims=True)
    weights = jnp.exp2((scores - peak) * EXP2_SCALE).astype(jnp.bfloat16)
    both = jnp.dot(weights, wide_ref[...], preferred_element_type=jnp.float32)
    return both[:, :HS], both[:, HS:], jnp.broadcast_to(peak, (TILE, HS))


def combine(found, ref):
    out, total = 0.0, 0.0
    for block_out, block_sum, peak in found:
        scale = jnp.exp2((peak - ref) * EXP2_SCALE)
        out = out + block_out * scale
        total = total + block_sum * scale
    return out, total


def query_tile(q_ref, step):
    return q_ref[:, 2 * step : 2 * step + 2].reshape(TILE, HS)


def attend_kernel(q_ref, own_ref, near_ref, out_ref, own_wide_ref, near_wide_ref):
    widen_into(own_wide_ref, own_ref)
    widen_into(near_wide_ref, near_ref)
    blocks = ((own_ref, own_wide_ref), (near_ref, near_wide_ref))
    biases = [bias_row(ref) for ref, _ in blocks]
    for step in range(TILES):
        q = query_tile(q_ref, step)
        found = [one_block(q, *block, bias) for block, bias in zip(blocks, biases)]
        peak = jnp.maximum(found[0][2], found[1][2])
        out, total = combine(found, peak)
        out_ref[0, step] = out
        out_ref[1, step] = total
        out_ref[2, step] = peak


def finish_kernel(
    q_ref, got_ref, far_ref, so_far_ref, resp_ref, out_ref, got_wide_ref, far_wide_ref
):
    widen_into(got_wide_ref, got_ref)
    widen_into(far_wide_ref, far_ref)
    got_bias, far_bias = bias_row(got_ref), bias_row(far_ref)
    resp = resp_ref[0:1]
    part = lane_ids((TILE, HS)) // PAIRS
    pair = lax.broadcasted_iota(jnp.int32, (4, PAIRS, HS), 1)
    diagonal = lane_ids((4, PAIRS, HS)) % PAIRS == pair
    sub = lax.broadcasted_iota(jnp.int32, (4, 8, HS), 1)

    def by_slot(x):
        x = x.reshape(8, 2, 8, HS)
        low, high = interleave(x[:, 0], x[:, 1])
        x = jnp.stack([low.reshape(2, 2, 2, 8, HS), high.reshape(2, 2, 2, 8, HS)], axis=1)
        return x.transpose(2, 1, 0, 3, 4, 5).reshape(4, PAIRS, HS)

    for step in range(TILES):
        q = query_tile(q_ref, step)
        found = [
            (so_far_ref[0, step], so_far_ref[1, step], so_far_ref[2, step]),
            one_block(q, got_ref, got_wide_ref, got_bias),
            one_block(q, far_ref, far_wide_ref, far_bias),
        ]
        ref = jnp.maximum(jnp.maximum(found[0][2], found[1][2]), found[2][2]).astype(jnp.bfloat16).astype(jnp.float32)
        out, total = combine(found, ref)
        high = total.astype(jnp.bfloat16).astype(jnp.float32)
        stats = jnp.where(part == 1, high, jnp.where(part == 2, total - high, resp))
        stats = jnp.where(part == 0, ref, stats)
        stats = jnp.where(diagonal, by_slot(stats), 0.0)
        stats = jnp.sum(stats, axis=1, keepdims=True)
        stats = jnp.where(sub == 0, stats, 0.0)
        full = jnp.concatenate([by_slot(out), stats], axis=1).reshape(4 * SLOT_ROWS, HS)
        place = (2 * step + FIRST_Y - LAST_Z) % NZ * 2 * SLOT_ROWS
        out_ref[place : place + 4 * SLOT_ROWS, :] = full.astype(jnp.bfloat16)


def merge_kernel(parts_ref, out_ref):
    parts = parts_ref[...].astype(jnp.float32).reshape(SRC, SLOT_ROWS, HS)
    resp = parts[0, PAIRS : PAIRS + 1, 3 * PAIRS : 3 * PAIRS + 1].astype(jnp.int32)
    stats = parts[:, PAIRS, :]
    stats = jnp.concatenate([stats, jnp.zeros((HS - SRC, HS), jnp.float32)], axis=0).T
    valid = lane_ids((PAIRS, HS)) < SRC
    peaks = jnp.where(valid, stats[:PAIRS], -jnp.inf)
    sums = stats[PAIRS : 2 * PAIRS] + stats[2 * PAIRS : 3 * PAIRS]
    peak = jnp.max(peaks, axis=1, keepdims=True)
    scale = jnp.exp2((peaks - peak) * EXP2_SCALE)
    denom = jnp.sum(scale * sums, axis=1, keepdims=True)
    numer = parts[0, :PAIRS] * scale[:, 0:1]
    for src in range(1, SRC):
        numer = numer + parts[src, :PAIRS] * scale[:, src : src + 1]
    result = numer / denom
    rows = PAIRS // 8
    row = lax.broadcasted_iota(jnp.int32, (rows, HS), 0)
    live = row + rows * lax.axis_index(("z", "x", "core")) < resp
    for place in range(8):
        block = result[rows * place : rows * (place + 1)]
        head = NC * HEAD_X[place // NC] + place % NC
        out_ref[:, HS * head : HS * (head + 1)] = jnp.where(live, block, 0.0).astype(jnp.bfloat16)


VMEM = pl.BlockSpec(memory_space=pltpu.VMEM)
SMEM = pl.BlockSpec(memory_space=pltpu.SMEM)
HBM = pl.BlockSpec(memory_space=pltpu.HBM)


def pack(counts, queries, keys, values):
    return pl.pallas_call(
        pack_kernel,
        out_shape=(
            jax.ShapeDtypeStruct((NZ, PAIRS, HS), jnp.bfloat16),
            jax.ShapeDtypeStruct((SEND_ROWS, HS), jnp.bfloat16),
        ),
        in_specs=[SMEM, HBM, HBM, HBM],
        out_specs=(HBM, HBM),
        scratch_shapes=[
            pltpu.VMEM((PAIRS, HS), jnp.bfloat16),
            pltpu.VMEM((NZ, PAIRS, HS), jnp.bfloat16),
            pltpu.VMEM((2 * SLOTS, HS), jnp.bfloat16),
            pltpu.VMEM((16, HS), jnp.bfloat16),
            pltpu.SemaphoreType.DMA((7,)),
        ],
        compiler_params=pltpu.CompilerParams(vmem_limit_bytes=60 * 2**20),
    )(counts, queries, keys, values)


def turn(resp_len, groups):
    return pl.pallas_call(
        turn_kernel,
        out_shape=(
            jax.ShapeDtypeStruct((2, NY, PAIRS, HS), jnp.bfloat16),
            jax.ShapeDtypeStruct((8, HS), jnp.float32),
        ),
        in_specs=[SMEM, VMEM],
        out_specs=(VMEM, VMEM),
        compiler_params=pltpu.CompilerParams(vmem_limit_bytes=2**20),
        cost_estimate=pl.CostEstimate(flops=2**36, bytes_accessed=2**21, transcendentals=0),
    )(resp_len, groups)


def attend(spread, own, near):
    return pl.pallas_call(
        attend_kernel,
        out_shape=jax.ShapeDtypeStruct((3, TILES, TILE, HS), jnp.float32),
        in_specs=[VMEM] * 3,
        out_specs=VMEM,
        scratch_shapes=[pltpu.VMEM((SLOTS, 2 * HS), jnp.bfloat16)] * 2,
        compiler_params=pltpu.CompilerParams(vmem_limit_bytes=12 * 2**20),
        cost_estimate=pl.CostEstimate(flops=2**34, bytes_accessed=2**21, transcendentals=0),
    )(spread, own, near)


def finish(spread, got, far, so_far, resp):
    return pl.pallas_call(
        finish_kernel,
        out_shape=jax.ShapeDtypeStruct((SRC * SLOT_ROWS, HS), jnp.bfloat16),
        in_specs=[VMEM] * 5,
        out_specs=VMEM,
        scratch_shapes=[pltpu.VMEM((SLOTS, 2 * HS), jnp.bfloat16)] * 2,
        compiler_params=pltpu.CompilerParams(vmem_limit_bytes=8 * 2**20),
    )(spread, got, far, so_far, resp)


def merge(parts):
    return pl.pallas_call(
        merge_kernel,
        out_shape=jax.ShapeDtypeStruct((4, 8 * HS), jnp.bfloat16),
        in_specs=[VMEM],
        out_specs=VMEM,
        compiler_params=pltpu.CompilerParams(vmem_limit_bytes=4 * 2**20),
    )(parts)


def local(queries, keys, values, counts, resp_len):
    swap_cores = [(0, 1), (1, 0)]
    swap_chips = [way for a, b in SHARERS for way in ((a, b), (b, a))]
    with jax.named_scope("query_spread"):
        slots, own = pack(counts, queries, keys, values)
        groups = exchange(slots.reshape(NZ * 4, 8, HS), groups_spread()).reshape(NZ, PAIRS, HS)
    with jax.named_scope("block_exchange"):
        near = lax.ppermute(own, "x", swap_chips)
        got = lax.ppermute(own, "core", swap_cores)
        far = lax.ppermute(near, "core", swap_cores)
    groups, own = lax.optimization_barrier((groups, own))
    with jax.named_scope("query_turn"):
        turned, resp = turn(resp_len, groups)
        spread = exchange(turned.reshape(SRC, PAIRS, HS), groups_turn()).reshape(2, NY, PAIRS, HS)
    with jax.named_scope("attend"):
        so_far = attend(spread, own, near)
        parts = finish(spread, got, far, so_far, resp)
    with jax.named_scope("merge"):
        parts = exchange(parts.reshape(SRC, SLOT_ROWS, HS), groups_merge())
        return merge(parts.reshape(SRC * SLOT_ROWS, HS))


def solution(mesh):
    grid = Mesh(mesh.devices.reshape(NZ, NX, NC, NY), ("z", "x", "core", "tp"))
    ctx = ("z", "x", "core")
    in_specs = (P("tp", ctx), P(ctx, "tp"), P(ctx, "tp"), P(ctx), P())
    return jax.shard_map(
        local, mesh=grid, in_specs=in_specs, out_specs=P(ctx, "tp"), check_vma=False
    )
```

```python
import jax
import jax.numpy as jnp
from jax import lax
from jax.experimental import pallas as pl
from jax.experimental.pallas import tpu as pltpu
from jax.sharding import Mesh, PartitionSpec as P

HS = 128
LOG2E = 1.4426950408889634
EXP2_SCALE = LOG2E / HS**0.5
NZ, NX, NC, NY = 8, 4, 2, 8
SLOTS = 1024
TILE = 128
TILES = 4
PAIRS = 32
SLOT_ROWS = 40
SRC = NZ * 2
SEND_ROWS = 2 * SLOTS + 16
COUNT_BASE = 64
MASKED = -1e30
FIRST_Z, FIRST_Y, LAST_Z = 5, 5, 5
SHARERS = ((0, 1), (3, 2))
CLASSES = ((3, 0), (2, 1))
HEAD_X = (3, 2, 0, 1)


def lane_ids(shape):
    return lax.broadcasted_iota(jnp.int32, shape, len(shape) - 1)


def device(z, x, core, y):
    return ((z % NZ * NX + x % NX) * NC + core) * NY + y % NY


def groups_spread():
    return [
        [device(z + FIRST_Z, x, core, y) for z in range(NZ) for x in pair for core in range(NC)]
        for pair in SHARERS
        for y in range(NY)
    ]


def groups_turn():
    return [
        [device(z, x, core, y + FIRST_Y) for x in pair for y in range(NY)]
        for z in range(NZ)
        for core in range(NC)
        for pair in CLASSES
    ]


def groups_merge():
    return [
        [device(z + LAST_Z, x, core, y) for z in range(NZ) for x in pair]
        for core in range(NC)
        for y in range(NY)
        for pair in CLASSES
    ]


def exchange(blocks, groups):
    axes = ("z", "x", "core", "tp")
    return lax.all_to_all(blocks, axes, 0, 0, axis_index_groups=groups, tiled=True)


def interleave(first, second):
    low = jnp.concatenate([first[:, :4], second[:, :4]], axis=1)
    high = jnp.concatenate([first[:, 4:], second[:, 4:]], axis=1)
    return low, high


def pack_kernel(
    count_ref, query_ref, key_ref, value_ref, slots_ref, send_ref, rows, slots, both, tail, sems
):
    def copy(source, target, which):
        made = pltpu.make_async_copy(source, target, sems.at[which])
        made.start()
        return made

    first, second = pl.ds(0, SLOTS), pl.ds(SLOTS, SLOTS)
    loads = (
        copy(query_ref, rows, 0),
        copy(key_ref, both.at[first], 1),
        copy(value_ref, both.at[second], 2),
    )
    loads[0].wait()
    by_x = rows[...].astype(jnp.float32).reshape(NX, 8, HS)
    parts = []
    for upper, lower in CLASSES:
        parts += interleave(by_x[upper : upper + 1], by_x[lower : lower + 1])
    block = jnp.concatenate(parts, axis=0).reshape(PAIRS, HS).astype(jnp.bfloat16)
    for z in range(NZ):
        slots[z] = block
    count = count_ref[0]
    row = lax.broadcasted_iota(jnp.int32, (16, HS), 0)
    high = count // COUNT_BASE
    tail[...] = jnp.where(row == 0, high, count - high * COUNT_BASE).astype(jnp.float32).astype(jnp.bfloat16)
    stores = [copy(slots, slots_ref, 3), copy(tail, send_ref.at[pl.ds(2 * SLOTS, 16)], 6)]
    for which, part in enumerate((first, second)):
        loads[1 + which].wait()
        stores.append(copy(both.at[part], send_ref.at[part], 4 + which))
    for store in stores:
        store.wait()


def turn_kernel(resp_ref, groups_ref, turned_ref, noted_ref):
    noted_ref[...] = jnp.full((8, HS), resp_ref[0], jnp.int32).astype(jnp.float32)
    for place in range(NY):
        block = groups_ref[(place + FIRST_Y - FIRST_Z) % NZ]
        for x in range(2):
            turned_ref[x, place] = block


def widen_into(wide_ref, ref):
    wide_ref[:, :HS] = ref[SLOTS : 2 * SLOTS, :]
    wide_ref[:, HS:] = jnp.ones((SLOTS, HS), jnp.bfloat16)


def tail_rows(ref):
    return ref[2 * SLOTS : SEND_ROWS, :].astype(jnp.float32)


def bias_row(ref):
    tail = tail_rows(ref)
    count = tail[0:1] * COUNT_BASE + tail[1:2]
    count = jnp.concatenate([count] * (SLOTS // HS), axis=1).astype(jnp.int32)
    return jnp.where(lane_ids((1, SLOTS)) < count, 0.0, MASKED)


def one_block(q, ref, wide_ref, bias):
    scores = lax.dot_general(
        q, ref[:SLOTS, :], (((1,), (1,)), ((), ())), preferred_element_type=jnp.float32
    )
    scores = scores + bias
    peak = jnp.max(scores, axis=1, keepdims=True)
    weights = jnp.exp2((scores - peak) * EXP2_SCALE).astype(jnp.bfloat16)
    both = jnp.dot(weights, wide_ref[...], preferred_element_type=jnp.float32)
    return both[:, :HS], both[:, HS:], jnp.broadcast_to(peak, (TILE, HS))


def combine(found, ref):
    out, total = 0.0, 0.0
    for block_out, block_sum, peak in found:
        scale = jnp.exp2((peak - ref) * EXP2_SCALE)
        out = out + block_out * scale
        total = total + block_sum * scale
    return out, total


def query_tile(q_ref, step):
    return q_ref[:, 2 * step : 2 * step + 2].reshape(TILE, HS)


def widen_kernel(own_ref, wide_ref):
    widen_into(wide_ref, own_ref)


def attend_kernel(q_ref, own_ref, own_wide_ref, near_ref, out_ref, near_wide_ref):
    widen_into(near_wide_ref, near_ref)
    blocks = ((own_ref, own_wide_ref), (near_ref, near_wide_ref))
    biases = [bias_row(ref) for ref, _ in blocks]
    for step in range(TILES):
        q = query_tile(q_ref, step)
        found = [one_block(q, *block, bias) for block, bias in zip(blocks, biases)]
        peak = jnp.maximum(found[0][2], found[1][2])
        out, total = combine(found, peak)
        out_ref[0, step] = out
        out_ref[1, step] = total
        out_ref[2, step] = peak


def finish_kernel(
    q_ref, got_ref, far_ref, so_far_ref, resp_ref, out_ref, got_wide_ref, far_wide_ref
):
    widen_into(got_wide_ref, got_ref)
    widen_into(far_wide_ref, far_ref)
    got_bias, far_bias = bias_row(got_ref), bias_row(far_ref)
    resp = resp_ref[0:1]
    part = lane_ids((TILE, HS)) // PAIRS
    pair = lax.broadcasted_iota(jnp.int32, (4, PAIRS, HS), 1)
    diagonal = lane_ids((4, PAIRS, HS)) % PAIRS == pair
    sub = lax.broadcasted_iota(jnp.int32, (4, 8, HS), 1)

    def by_slot(x):
        x = x.reshape(8, 2, 8, HS)
        low, high = interleave(x[:, 0], x[:, 1])
        x = jnp.stack([low.reshape(2, 2, 2, 8, HS), high.reshape(2, 2, 2, 8, HS)], axis=1)
        return x.transpose(2, 1, 0, 3, 4, 5).reshape(4, PAIRS, HS)

    for step in range(TILES):
        q = query_tile(q_ref, step)
        found = [
            (so_far_ref[0, step], so_far_ref[1, step], so_far_ref[2, step]),
            one_block(q, got_ref, got_wide_ref, got_bias),
            one_block(q, far_ref, far_wide_ref, far_bias),
        ]
        ref = jnp.maximum(jnp.maximum(found[0][2], found[1][2]), found[2][2]).astype(jnp.bfloat16).astype(jnp.float32)
        out, total = combine(found, ref)
        high = total.astype(jnp.bfloat16).astype(jnp.float32)
        stats = jnp.where(part == 1, high, jnp.where(part == 2, total - high, resp))
        stats = jnp.where(part == 0, ref, stats)
        stats = jnp.where(diagonal, by_slot(stats), 0.0)
        stats = jnp.sum(stats, axis=1, keepdims=True)
        stats = jnp.where(sub == 0, stats, 0.0)
        full = jnp.concatenate([by_slot(out), stats], axis=1).reshape(4 * SLOT_ROWS, HS)
        place = (2 * step + FIRST_Y - LAST_Z) % NZ * 2 * SLOT_ROWS
        out_ref[place : place + 4 * SLOT_ROWS, :] = full.astype(jnp.bfloat16)


def merge_kernel(parts_ref, out_ref):
    parts = parts_ref[...].astype(jnp.float32).reshape(SRC, SLOT_ROWS, HS)
    resp = parts[0, PAIRS : PAIRS + 1, 3 * PAIRS : 3 * PAIRS + 1].astype(jnp.int32)
    stats = parts[:, PAIRS, :]
    stats = jnp.concatenate([stats, jnp.zeros((HS - SRC, HS), jnp.float32)], axis=0).T
    valid = lane_ids((PAIRS, HS)) < SRC
    peaks = jnp.where(valid, stats[:PAIRS], -jnp.inf)
    sums = stats[PAIRS : 2 * PAIRS] + stats[2 * PAIRS : 3 * PAIRS]
    peak = jnp.max(peaks, axis=1, keepdims=True)
    scale = jnp.exp2((peaks - peak) * EXP2_SCALE)
    denom = jnp.sum(scale * sums, axis=1, keepdims=True)
    numer = parts[0, :PAIRS] * scale[:, 0:1]
    for src in range(1, SRC):
        numer = numer + parts[src, :PAIRS] * scale[:, src : src + 1]
    result = numer / denom
    rows = PAIRS // 8
    row = lax.broadcasted_iota(jnp.int32, (rows, HS), 0)
    live = row + rows * lax.axis_index(("z", "x", "core")) < resp
    for place in range(8):
        block = result[rows * place : rows * (place + 1)]
        head = NC * HEAD_X[place // NC] + place % NC
        out_ref[:, HS * head : HS * (head + 1)] = jnp.where(live, block, 0.0).astype(jnp.bfloat16)


VMEM = pl.BlockSpec(memory_space=pltpu.VMEM)
SMEM = pl.BlockSpec(memory_space=pltpu.SMEM)
HBM = pl.BlockSpec(memory_space=pltpu.HBM)


def pack(counts, queries, keys, values):
    return pl.pallas_call(
        pack_kernel,
        out_shape=(
            jax.ShapeDtypeStruct((NZ, PAIRS, HS), jnp.bfloat16),
            jax.ShapeDtypeStruct((SEND_ROWS, HS), jnp.bfloat16),
        ),
        in_specs=[SMEM, HBM, HBM, HBM],
        out_specs=(HBM, HBM),
        scratch_shapes=[
            pltpu.VMEM((PAIRS, HS), jnp.bfloat16),
            pltpu.VMEM((NZ, PAIRS, HS), jnp.bfloat16),
            pltpu.VMEM((2 * SLOTS, HS), jnp.bfloat16),
            pltpu.VMEM((16, HS), jnp.bfloat16),
            pltpu.SemaphoreType.DMA((7,)),
        ],
        compiler_params=pltpu.CompilerParams(vmem_limit_bytes=60 * 2**20),
    )(counts, queries, keys, values)


def turn(resp_len, groups):
    return pl.pallas_call(
        turn_kernel,
        out_shape=(
            jax.ShapeDtypeStruct((2, NY, PAIRS, HS), jnp.bfloat16),
            jax.ShapeDtypeStruct((8, HS), jnp.float32),
        ),
        in_specs=[SMEM, VMEM],
        out_specs=(VMEM, VMEM),
        compiler_params=pltpu.CompilerParams(vmem_limit_bytes=2**20),
        cost_estimate=pl.CostEstimate(flops=2**36, bytes_accessed=2**21, transcendentals=0),
    )(resp_len, groups)


def widen(own):
    return pl.pallas_call(
        widen_kernel,
        out_shape=jax.ShapeDtypeStruct((SLOTS, 2 * HS), jnp.bfloat16),
        in_specs=[VMEM],
        out_specs=VMEM,
        compiler_params=pltpu.CompilerParams(vmem_limit_bytes=2**20),
    )(own)


def attend(spread, own, own_wide, near):
    return pl.pallas_call(
        attend_kernel,
        out_shape=jax.ShapeDtypeStruct((3, TILES, TILE, HS), jnp.float32),
        in_specs=[VMEM] * 4,
        out_specs=VMEM,
        scratch_shapes=[pltpu.VMEM((SLOTS, 2 * HS), jnp.bfloat16)],
        compiler_params=pltpu.CompilerParams(vmem_limit_bytes=12 * 2**20),
        cost_estimate=pl.CostEstimate(flops=2**34, bytes_accessed=2**21, transcendentals=0),
    )(spread, own, own_wide, near)


def finish(spread, got, far, so_far, resp):
    return pl.pallas_call(
        finish_kernel,
        out_shape=jax.ShapeDtypeStruct((SRC * SLOT_ROWS, HS), jnp.bfloat16),
        in_specs=[VMEM] * 5,
        out_specs=VMEM,
        scratch_shapes=[pltpu.VMEM((SLOTS, 2 * HS), jnp.bfloat16)] * 2,
        compiler_params=pltpu.CompilerParams(vmem_limit_bytes=8 * 2**20),
    )(spread, got, far, so_far, resp)


def merge(parts):
    return pl.pallas_call(
        merge_kernel,
        out_shape=jax.ShapeDtypeStruct((4, 8 * HS), jnp.bfloat16),
        in_specs=[VMEM],
        out_specs=VMEM,
        compiler_params=pltpu.CompilerParams(vmem_limit_bytes=4 * 2**20),
    )(parts)


def local(queries, keys, values, counts, resp_len):
    swap_cores = [(0, 1), (1, 0)]
    swap_chips = [way for a, b in SHARERS for way in ((a, b), (b, a))]
    with jax.named_scope("query_spread"):
        slots, own = pack(counts, queries, keys, values)
        groups = exchange(slots.reshape(NZ * 4, 8, HS), groups_spread()).reshape(NZ, PAIRS, HS)
    with jax.named_scope("block_exchange"):
        near = lax.ppermute(own, "x", swap_chips)
        got = lax.ppermute(own, "core", swap_cores)
        far = lax.ppermute(near, "core", swap_cores)
    groups, own = lax.optimization_barrier((groups, own))
    with jax.named_scope("query_turn"):
        turned, resp = turn(resp_len, groups)
        spread = exchange(turned.reshape(SRC, PAIRS, HS), groups_turn()).reshape(2, NY, PAIRS, HS)
    with jax.named_scope("attend"):
        so_far = attend(spread, own, widen(own), near)
        parts = finish(spread, got, far, so_far, resp)
    with jax.named_scope("merge"):
        parts = exchange(parts.reshape(SRC, SLOT_ROWS, HS), groups_merge())
        return merge(parts.reshape(SRC * SLOT_ROWS, HS))


def solution(mesh):
    grid = Mesh(mesh.devices.reshape(NZ, NX, NC, NY), ("z", "x", "core", "tp"))
    ctx = ("z", "x", "core")
    in_specs = (P("tp", ctx), P(ctx, "tp"), P(ctx, "tp"), P(ctx), P())
    return jax.shard_map(
        local, mesh=grid, in_specs=in_specs, out_specs=P(ctx, "tp"), check_vma=False
    )
```
